32 devices in a mesh: gx: 8 (over y, x, core), gy: 4 (over z).
Axes of the slice: x: 2, y: 2, z: 4, core: 2. Of those that a mesh axis runs over, the one named last changes fastest.
Arguments:
- stress: float32 [6, 16, 512, 512], P(None, None, 'gx', 'gy'), may hold values from -6 to 6
- velocity: float32 [3, 16, 512, 512], P(None, None, 'gx', 'gy'), may hold values from -6 to 6
- material: int32 [16, 512, 512], P(None, 'gx', 'gy'), may hold values from 0 to 2
- layer_kind: int32 [16], replicated, may hold values from 0 to 2
- buoyancy: float32 [3], replicated, may hold values from 0.05 to 0.3
- lame_first: float32 [3], replicated, may hold values from 0.05 to 0.3
- shear_modulus: float32 [3], replicated, may hold values from 0.05 to 0.2
- piezo: float32 [3], replicated, may hold values from 0.5 to 2
- permit_lateral: float32 [3], replicated, may hold values from 0.5 to 4
- permit_normal: float32 [3], replicated, may hold values from 0.5 to 4
Outputs:
- stress_next: float32 [6, 16, 512, 512], P(None, None, 'gx', 'gy')
- velocity_next: float32 [3, 16, 512, 512], P(None, None, 'gx', 'gy')
- potential_modes: float32 [2, 16, 512, 512], P(None, None, ('gx', 'gy'))
The draws below stay inside these ranges and needn't reach their ends.
Inputs may be any that keep to these rules, and one draw needn't show every extreme that they name: `layer_kind`: material codes of the layers, as for cells.
All inputs are finite; a program needn't handle non-finite values.
Results may differ from the reference program's by a relative error of at most 0.000076.
Values sent between devices are 32-bit elements; how exact they have to be, the bound alone decides.
A program may use at most 192 MiB of HBM per device.

```python
import math
import jax
import jax.numpy as jnp

NZ = 16
NX = 512
NY = 512


def plant(values, rng, low, high):
    longest = values.shape.index(max(values.shape))
    spots = []
    for shift in (0, 1):
        where = [jax.random.randint(jax.random.fold_in(rng, axis), (), 0, length) for axis, length in enumerate(values.shape)]
        where[longest] = (where[longest] + shift) % values.shape[longest]
        spots.append(tuple(where))
    return values.at[spots[0]].set(low).at[spots[1]].set(high)


def block_levels(key, extent, cuts, low, high):
    gain, own = 1.0, jax.random.fold_in(key, 6)
    for position, blocks in cuts:
        heights = jnp.exp(jax.random.uniform(jax.random.fold_in(own, position), (blocks,), jnp.float32, low / len(cuts), high / len(cuts)))
        gain = gain * jnp.repeat(heights, extent[position] // blocks).reshape([-1 if axis == position else 1 for axis in range(len(extent))])
    return gain


def noise(key, extent, scale, bound, shards=(), kind=jnp.bfloat16):
    entries = scale * jax.random.normal(key, extent, jnp.float32)
    if shards:
        entries = entries * block_levels(key, extent, shards, -0.22, 0.18)
    return jnp.clip(entries, -bound, bound).astype(kind)


def setup_inputs(seed: int = 0) -> dict:
    streams_of = jax.random.split(jax.random.key(seed), 11)
    stress = noise(streams_of[0], (6, NZ, NX, NY), 1.0, 6.0, ((2, 8), (3, 4)), jnp.float32)
    velocity = noise(streams_of[1], (3, NZ, NX, NY), 1.0, 6.0, ((2, 8), (3, 4)), jnp.float32)
    material = plant(jax.random.randint(streams_of[2], (NZ, NX, NY), 0, 3), jax.random.fold_in(streams_of[2], 1), 0, 2).astype(jnp.int32)
    layer_kind = plant(jax.random.randint(streams_of[3], (NZ,), 0, 3), jax.random.fold_in(streams_of[3], 1), 0, 2).astype(jnp.int32)
    buoyancy = jnp.clip(jnp.exp(jax.random.uniform(streams_of[4], (3,), jnp.float32, math.log(0.05), math.log(0.3))), 0.05, 0.3)
    lame_first = jnp.clip(jnp.exp(jax.random.uniform(streams_of[5], (3,), jnp.float32, math.log(0.05), math.log(0.3))), 0.05, 0.3)
    shear_modulus = jnp.clip(jnp.exp(jax.random.uniform(streams_of[6], (3,), jnp.float32, math.log(0.05), math.log(0.2))), 0.05, 0.2)
    piezo = jnp.clip(jnp.exp(jax.random.uniform(streams_of[7], (3,), jnp.float32, math.log(0.5), math.log(2.0))), 0.5, 2.0)
    permit_lateral = jnp.clip(jnp.exp(jax.random.uniform(streams_of[8], (3,), jnp.float32, math.log(0.5), math.log(4.0))), 0.5, 4.0)
    permit_normal = jnp.clip(jnp.exp(jax.random.uniform(streams_of[9], (3,), jnp.float32, math.log(0.5), math.log(4.0))), 0.5, 4.0)
    return {"stress": stress, "velocity": velocity, "material": material, "layer_kind": layer_kind, "buoyancy": buoyancy, "lame_first": lame_first, "shear_modulus": shear_modulus, "piezo": piezo, "permit_lateral": permit_lateral, "permit_normal": permit_normal}


def lookup(codes, table):
    result = jnp.zeros(codes.shape, jnp.float32)
    for material_no in range(3):
        result = result + jnp.where(codes == material_no, table[material_no], 0.0)
    return result


def centre(padded):
    return padded[..., 1:-1, 1:-1]


def x_plus(padded):
    return padded[..., 2:, 1:-1] - padded[..., 1:-1, 1:-1]


def x_minus(padded):
    return padded[..., 1:-1, 1:-1] - padded[..., :-2, 1:-1]


def y_plus(padded):
    return padded[..., 1:-1, 2:] - padded[..., 1:-1, 1:-1]


def y_minus(padded):
    return padded[..., 1:-1, 1:-1] - padded[..., 1:-1, :-2]


def z_plus(inner):
    upper = jnp.concatenate([inner[1:], jnp.zeros_like(inner[:1])], axis=0)
    return upper - inner


def z_minus(inner):
    lower = jnp.concatenate([jnp.zeros_like(inner[:1]), inner[:-1]], axis=0)
    return inner - lower


def advance_velocity(stress_pad, veloc, buoy_field):
    new_x = veloc[0] + buoy_field * (x_plus(stress_pad[0]) + y_minus(stress_pad[3]) + z_minus(centre(stress_pad[4])))
    new_y = veloc[1] + buoy_field * (x_minus(stress_pad[3]) + y_plus(stress_pad[1]) + z_minus(centre(stress_pad[5])))
    new_z = veloc[2] + buoy_field * (x_minus(stress_pad[4]) + y_minus(stress_pad[5]) + z_plus(centre(stress_pad[2])))
    return jnp.stack([new_x, new_y, new_z])


def advance_stress(stress, veloc_pad, lame_field, shear_field):
    strain_x = x_minus(veloc_pad[0])
    strain_y = y_minus(veloc_pad[1])
    strain_z = z_minus(centre(veloc_pad[2]))
    diverge = strain_x + strain_y + strain_z
    new_xx = stress[0] + lame_field * diverge + 2.0 * shear_field * strain_x
    new_yy = stress[1] + lame_field * diverge + 2.0 * shear_field * strain_y
    new_zz = stress[2] + lame_field * diverge + 2.0 * shear_field * strain_z
    new_xy = stress[3] + shear_field * (y_plus(veloc_pad[0]) + x_plus(veloc_pad[1]))
    new_xz = stress[4] + shear_field * (z_plus(centre(veloc_pad[0])) + x_plus(veloc_pad[2]))
    new_yz = stress[5] + shear_field * (z_plus(centre(veloc_pad[1])) + y_plus(veloc_pad[2]))
    return jnp.stack([new_xx, new_yy, new_zz, new_xy, new_xz, new_yz])


def couplings(layer_kind, permit_lateral, permit_normal):
    lateral = lookup(layer_kind, permit_lateral)
    normal = lookup(layer_kind, permit_normal)
    couple = jnp.concatenate([normal[:1], 0.5 * (normal[:-1] + normal[1:]), normal[-1:]])
    return lateral, couple


def solve_layers(rhs, wave, lateral, couple):
    layers = rhs.shape[1]
    factors = []
    carries = []
    for layer_no in range(layers):
        pivot = couple[layer_no] + couple[layer_no + 1] + wave * lateral[layer_no]
        if layer_no > 0:
            pivot = pivot - couple[layer_no] * factors[-1]
            carry = (rhs[:, layer_no] + couple[layer_no] * carries[-1]) / pivot
        else:
            carry = rhs[:, layer_no] / pivot
        factors.append(couple[layer_no + 1] / pivot)
        carries.append(carry)
    solved = [carries[-1]]
    for layer_no in range(layers - 2, -1, -1):
        solved.append(carries[layer_no] + factors[layer_no] * solved[-1])
    return jnp.stack(solved[::-1], axis=1)


def pad_xy(array):
    widths = [(0, 0)] * (array.ndim - 2) + [(1, 1), (1, 1)]
    return jnp.pad(array, widths)


def reference(stress, velocity, material, layer_kind, buoyancy, lame_first, shear_modulus, piezo, permit_lateral, permit_normal):
    buoy_field = lookup(material, buoyancy)
    lame_field = lookup(material, lame_first)
    shear_field = lookup(material, shear_modulus)
    velocity_next = advance_velocity(pad_xy(stress), velocity, buoy_field)
    stress_next = advance_stress(stress, pad_xy(velocity_next), lame_field, shear_field)
    charge = lookup(material, piezo) * (stress_next[4] + stress_next[5])
    spectrum = jnp.fft.fft2(charge, axes=(1, 2), norm="ortho")
    rhs = jnp.stack([jnp.real(spectrum), jnp.imag(spectrum)]).astype(jnp.float32)
    rhs = jnp.transpose(rhs, (0, 1, 3, 2))
    wave_x = 2.0 * jnp.sin(math.pi * jnp.arange(NX, dtype=jnp.int32).astype(jnp.float32) / NX)
    wave_y = 2.0 * jnp.sin(math.pi * jnp.arange(NY, dtype=jnp.int32).astype(jnp.float32) / NY)
    wave = wave_y[:, None] * wave_y[:, None] + wave_x[None, :] * wave_x[None, :]
    lateral, couple = couplings(layer_kind, permit_lateral, permit_normal)
    potential_modes = solve_layers(rhs, wave, lateral, couple)
    return stress_next, velocity_next, potential_modes
```

```python
import functools
import math

import jax
import jax.numpy as jnp
import ml_dtypes
import numpy as np
from jax import lax
from jax.experimental import pallas as pl
from jax.experimental.pallas import tpu as pltpu
from jax.sharding import PartitionSpec as P

MESH = pl.DeviceIdType.MESH
F32 = jnp.float32
BF16 = jnp.bfloat16


def split_table(table):
    high = table.astype(np.float32).astype(ml_dtypes.bfloat16)
    low = (table - high.astype(np.float64)).astype(np.float32).astype(ml_dtypes.bfloat16)
    return high, low


@functools.lru_cache(maxsize=2)
def tables_y(count_x, count_y, total_y):
    block = total_y // (count_x * count_y)
    place = np.arange(total_y)
    angle = 2.0 * np.pi / total_y * (place[:, None] * place[None, :] % total_y)
    both = np.stack([np.cos(angle), -np.sin(angle)], axis=1) / math.sqrt(total_y)
    both = both.reshape(total_y, 2, count_x, count_y, block).transpose(2, 0, 3, 1, 4)
    return split_table(both.reshape(count_x, total_y, count_y * 2 * block))


@functools.lru_cache(maxsize=2)
def tables_x(total_x):
    place = np.arange(total_x)
    angle = 2.0 * np.pi / total_x * (place[:, None] * place[None, :] % total_x)
    scale = 1.0 / math.sqrt(total_x)
    return split_table(np.cos(angle) * scale) + split_table(np.sin(angle) * scale)


def pick(codes, table):
    return jnp.where(codes == 0, table[0], jnp.where(codes == 1, table[1], table[2]))


def dot3(a_high, a_low, b_high, b_low):
    dot = functools.partial(jnp.dot, preferred_element_type=F32)
    return dot(a_high, b_high) + (dot(a_high, b_low) + dot(a_low, b_high))


def step_kernel(
    nx, ny,
    buoy_t, lame_t, shear_t, piezo_t,
    stress_in, veloc_in, mat_in, thigh_in, tlow_in,
    stress_out, veloc_out, lines_out,
    s_ref, v_ref, m_ref, thigh, tlow,
    xs, xr, ys, yr, charge, cols, chigh, clow, sendbuf,
    in_sem, out_sem, hsend, hrecv, a_send, a_recv, b_send, b_recv,
):
    gx, gy = lax.axis_index("gx"), lax.axis_index("gy")
    me = gx * ny + gy
    total = nx * ny
    nz, cx, cy = m_ref.shape
    zc = nz // ny
    width = lines_out.shape[2] // zc

    loads = [
        pltpu.make_async_copy(src, dst, in_sem.at[no])
        for no, (src, dst) in enumerate(
            [(stress_in, s_ref), (veloc_in, v_ref), (mat_in, m_ref), (thigh_in, thigh), (tlow_in, tlow)]
        )
    ]
    for load in loads:
        load.start()

    barrier = pltpu.get_barrier_semaphore()

    def greet(step, carry):
        other = lax.rem(me + step, total)
        pl.semaphore_signal(
            barrier, inc=1, device_id=(other // ny, lax.rem(other, ny)), device_id_type=MESH
        )
        return carry

    lax.fori_loop(1, total, greet, 0)

    row = lax.broadcasted_iota(jnp.int32, (cx, cy), 0)
    lane = lax.broadcasted_iota(jnp.int32, (cx, cy), 1)

    def to_lane(value, source, target):
        return pltpu.roll(value, lax.rem(target - source + cy, cy), 1)

    has = (gx > 0, gx < nx - 1, gy > 0, gy < ny - 1)
    targets = ((gx - 1, gy), (gx + 1, gy), (gx, gy - 1), (gx, gy + 1))
    opposite = (1, 0, 3, 2)

    def halo_copy(turn, side):
        send, recv = (xs, xr) if side < 2 else (ys, yr)
        slot = turn * 2 + side % 2
        return pltpu.make_async_remote_copy(
            src_ref=send.at[slot],
            dst_ref=recv.at[slot],
            send_sem=hsend.at[turn * 4 + side],
            recv_sem=hrecv.at[turn * 4 + side],
            device_id=targets[side],
            device_id_type=MESH,
        )

    def halo_start(turn):
        for side in range(4):
            @pl.when(has[side])
            def _():
                halo_copy(turn, side).start()

    def halo_wait(turn):
        for side in range(4):
            @pl.when(has[side])
            def _():
                halo_copy(turn, side).wait_send()

            @pl.when(has[opposite[side]])
            def _():
                halo_copy(turn, side).wait_recv()

    for side in range(4):
        recv = xr if side < 2 else yr
        for turn in range(2):
            @pl.when(jnp.logical_not(has[opposite[side]]))
            def _():
                recv[turn * 2 + side % 2] = jnp.zeros(recv.shape[1:], F32)

    loads[0].wait()
    xs[0, 0] = s_ref[0, :, 0, :]
    xs[0, 1] = jnp.zeros((nz, cy), F32)
    xs[1, 0] = s_ref[3, :, cx - 1, :]
    xs[1, 1] = s_ref[4, :, cx - 1, :]

    def pack_stress(z, carry):
        low, high = carry
        low = jnp.where(lane == z, to_lane(s_ref[1, z], 0, z), low)
        high = jnp.where(lane == z, to_lane(s_ref[3, z], cy - 1, z), high)
        high = jnp.where(lane == nz + z, to_lane(s_ref[5, z], cy - 1, nz + z), high)
        return low, high

    empty = jnp.zeros((cx, cy), F32)
    low, high = lax.fori_loop(0, nz, pack_stress, (empty, empty))
    ys[0] = low
    ys[1] = high
    pl.semaphore_wait(barrier, total - 1)
    halo_start(0)
    loads[1].wait()
    loads[2].wait()
    halo_wait(0)

    def x_next(value, turn, item, z):
        edge = xr[turn * 2, item, pl.ds(z, 1), :]
        return jnp.where(row == cx - 1, edge, pltpu.roll(value, cx - 1, 0))

    def x_last(value, turn, item, z):
        edge = xr[turn * 2 + 1, item, pl.ds(z, 1), :]
        return jnp.where(row == 0, edge, pltpu.roll(value, 1, 0))

    def y_next(value, turn, item, z):
        edge = to_lane(yr[turn * 2], item * nz + z, cy - 1)
        return jnp.where(lane == cy - 1, edge, pltpu.roll(value, cy - 1, 1))

    def y_last(value, turn, item, z):
        edge = to_lane(yr[turn * 2 + 1], item * nz + z, 0)
        return jnp.where(lane == 0, edge, pltpu.roll(value, 1, 1))

    def above(ref, item, z):
        return jnp.where(z < nz - 1, ref[item, jnp.minimum(z + 1, nz - 1)], 0.0)

    def below(ref, item, z):
        return jnp.where(z > 0, ref[item, jnp.maximum(z - 1, 0)], 0.0)

    def move(z, carry):
        low, high = carry
        buoy = pick(m_ref[z], buoy_t)
        sxx, syy, szz, sxy, sxz, syz = (s_ref[item, z] for item in range(6))
        ux = v_ref[0, z] + buoy * (
            (x_next(sxx, 0, 0, z) - sxx) + (sxy - y_last(sxy, 0, 0, z)) + (sxz - below(s_ref, 4, z))
        )
        uy = v_ref[1, z] + buoy * (
            (sxy - x_last(sxy, 0, 0, z)) + (y_next(syy, 0, 0, z) - syy) + (syz - below(s_ref, 5, z))
        )
        uz = v_ref[2, z] + buoy * (
            (sxz - x_last(sxz, 0, 1, z)) + (syz - y_last(syz, 0, 1, z)) + (above(s_ref, 2, z) - szz)
        )
        v_ref[0, z] = ux
        v_ref[1, z] = uy
        v_ref[2, z] = uz
        low = jnp.where(lane == z, to_lane(ux, 0, z), low)
        low = jnp.where(lane == nz + z, to_lane(uz, 0, nz + z), low)
        high = jnp.where(lane == z, to_lane(uy, cy - 1, z), high)
        return low, high

    low, high = lax.fori_loop(0, nz, move, (empty, empty))
    xs[2, 0] = v_ref[1, :, 0, :]
    xs[2, 1] = v_ref[2, :, 0, :]
    xs[3, 0] = v_ref[0, :, cx - 1, :]
    xs[3, 1] = jnp.zeros((nz, cy), F32)
    ys[2] = low
    ys[3] = high
    halo_start(1)
    save_veloc = pltpu.make_async_copy(v_ref, veloc_out, out_sem.at[0])
    save_veloc.start()
    halo_wait(1)

    def strain(z, carry):
        mat = m_ref[z]
        lame, shear, piezo = pick(mat, lame_t), pick(mat, shear_t), pick(mat, piezo_t)
        ux, uy, uz = v_ref[0, z], v_ref[1, z], v_ref[2, z]
        strain_x = ux - x_last(ux, 1, 0, z)
        strain_y = uy - y_last(uy, 1, 0, z)
        strain_z = uz - below(v_ref, 2, z)
        spread = lame * (strain_x + strain_y + strain_z)
        twice = 2.0 * shear
        s_ref[0, z] = s_ref[0, z] + spread + twice * strain_x
        s_ref[1, z] = s_ref[1, z] + spread + twice * strain_y
        s_ref[2, z] = s_ref[2, z] + spread + twice * strain_z
        s_ref[3, z] = s_ref[3, z] + shear * (
            (y_next(ux, 1, 0, z) - ux) + (x_next(uy, 1, 0, z) - uy)
        )
        sxz = s_ref[4, z] + shear * ((above(v_ref, 0, z) - ux) + (x_next(uz, 1, 1, z) - uz))
        syz = s_ref[5, z] + shear * ((above(v_ref, 1, z) - uy) + (y_next(uz, 1, 1, z) - uz))
        s_ref[4, z] = sxz
        s_ref[5, z] = syz
        charge[z] = piezo * (sxz + syz)
        return carry

    def line_copy(other):
        return pltpu.make_async_remote_copy(
            src_ref=charge.at[pl.ds(other * zc, zc)],
            dst_ref=cols.at[gy],
            send_sem=a_send.at[other],
            recv_sem=a_recv.at[gy],
            device_id=(gx, other),
            device_id_type=MESH,
        )

    def arrived_line(other):
        return pltpu.make_async_remote_copy(
            src_ref=charge.at[pl.ds(other * zc, zc)],
            dst_ref=cols.at[other],
            send_sem=a_send.at[other],
            recv_sem=a_recv.at[other],
            device_id=(gx, other),
            device_id_type=MESH,
        )

    def chunk(step, carry):
        other = lax.rem(gy + step, ny)
        lax.fori_loop(other * zc, other * zc + zc, strain, 0)
        line_copy(other).start()
        return carry

    lax.fori_loop(1, ny, chunk, 0)
    lax.fori_loop(gy * zc, gy * zc + zc, strain, 0)
    save_stress = pltpu.make_async_copy(s_ref, stress_out, out_sem.at[1])
    save_stress.start()

    def store_cols(source, value):
        flat = value.reshape(zc * cx, cy)
        high = flat.astype(BF16)
        where = pl.ds(pl.multiple_of(source * cy, cy), cy)
        chigh[:, where] = high
        clow[:, where] = (flat - high.astype(F32)).astype(BF16)

    store_cols(gy, charge[pl.ds(gy * zc, zc)])

    def take_cols(step, carry):
        source = lax.rem(gy - step + ny, ny)
        arrived_line(source).wait_recv()
        store_cols(source, cols[source])
        return carry

    lax.fori_loop(1, ny, take_cols, 0)
    loads[3].wait()
    loads[4].wait()

    def block_copy(other):
        return pltpu.make_async_remote_copy(
            src_ref=sendbuf.at[other],
            dst_ref=lines_out.at[gy, pl.ds(pl.multiple_of(gx * cx, cx), cx), :],
            send_sem=b_send.at[other],
            recv_sem=b_recv.at[me],
            device_id=(other // ny, lax.rem(other, ny)),
            device_id_type=MESH,
        )

    def arrived_block(other):
        sx, sy = other // ny, lax.rem(other, ny)
        return pltpu.make_async_remote_copy(
            src_ref=sendbuf.at[other],
            dst_ref=lines_out.at[sy, pl.ds(pl.multiple_of(sx * cx, cx), cx), :],
            send_sem=b_send.at[other],
            recv_sem=b_recv.at[other],
            device_id=(sx, sy),
            device_id_type=MESH,
        )

    def transform(step, carry):
        target_x = lax.rem(gx + step, nx)
        value = dot3(chigh[...], clow[...], thigh[target_x], tlow[target_x])
        for target_y in range(ny):
            other = target_x * ny + target_y
            sendbuf[other] = jnp.concatenate(
                [
                    value[z * cx : (z + 1) * cx, target_y * width : (target_y + 1) * width]
                    for z in range(zc)
                ],
                axis=1,
            )
        for target_y in range(ny):
            other = target_x * ny + target_y

            @pl.when(other != me)
            def _():
                block_copy(other).start()

        return carry

    lax.fori_loop(1, nx + 1, transform, 0)
    own = pltpu.make_async_copy(
        sendbuf.at[me],
        lines_out.at[gy, pl.ds(pl.multiple_of(gx * cx, cx), cx), :],
        out_sem.at[2],
    )
    own.start()

    def finish_lines(step, carry):
        line_copy(lax.rem(gy + step, ny)).wait_send()
        return carry

    lax.fori_loop(1, ny, finish_lines, 0)

    def finish_blocks(step, carry):
        other = lax.rem(me + step, total)
        block_copy(other).wait_send()
        arrived_block(other).wait_recv()
        return carry

    lax.fori_loop(1, total, finish_blocks, 0)
    own.wait()
    save_veloc.wait()
    save_stress.wait()


def solve_kernel(
    ny, kinds, lateral_t, normal_t,
    lines, cos_high, cos_low, sin_high, sin_low, wave_x, wave_y,
    modes, high, low,
):
    me = lax.axis_index("gx") * ny + lax.axis_index("gy")
    width = lines.shape[2]
    _, nz, block, _ = modes.shape

    @pl.when(pl.program_id(0) == 0)
    def _():
        for source in range(ny):
            value = lines[source].T
            top = value.astype(BF16)
            high[source * width : (source + 1) * width, :] = top
            low[source * width : (source + 1) * width, :] = (value - top.astype(F32)).astype(BF16)

    with_cos = dot3(high[...], low[...], cos_high[...], cos_low[...])
    with_sin = dot3(high[...], low[...], sin_high[...], sin_low[...])

    def part(value, z, no):
        start = (z * 2 + no) * block
        return value[start : start + block]

    lateral = [pick(kinds[z], lateral_t) for z in range(nz)]
    normal = [pick(kinds[z], normal_t) for z in range(nz)]
    couple = [normal[0]] + [0.5 * (normal[z - 1] + normal[z]) for z in range(1, nz)] + [normal[-1]]
    wave = wave_y[me][:, :1] + wave_x[...]
    factors, reals, imags = [], [], []
    for z in range(nz):
        real = part(with_cos, z, 0) + part(with_sin, z, 1)
        imag = part(with_cos, z, 1) - part(with_sin, z, 0)
        pivot = couple[z] + couple[z + 1] + wave * lateral[z]
        if z > 0:
            pivot = pivot - couple[z] * factors[-1]
            real = real + couple[z] * reals[-1]
            imag = imag + couple[z] * imags[-1]
        inverse = 1.0 / pivot
        factors.append(couple[z + 1] * inverse)
        reals.append(real * inverse)
        imags.append(imag * inverse)
    real, imag = reals[-1], imags[-1]
    for z in range(nz - 1, -1, -1):
        if z < nz - 1:
            real = reals[z] + factors[z] * real
            imag = imags[z] + factors[z] * imag
        modes[0, z] = real
        modes[1, z] = imag


def per_device(
    nx, ny, stress, velocity, material, layer_kind,
    buoyancy, lame_first, shear_modulus, piezo, permit_lateral, permit_normal,
):
    nz, cx, cy = material.shape
    total_x, total_y = cx * nx, cy * ny
    total = nx * ny
    block = total_y // total
    zc = nz // ny
    width = zc * 2 * block
    smem = pl.BlockSpec(memory_space=pltpu.SMEM)
    hbm = pl.BlockSpec(memory_space=pl.ANY)
    thigh, tlow = tables_y(nx, ny, total_y)
    stress_next, velocity_next, lines = pl.pallas_call(
        functools.partial(step_kernel, nx, ny),
        out_shape=(
            jax.ShapeDtypeStruct(stress.shape, F32),
            jax.ShapeDtypeStruct(velocity.shape, F32),
            jax.ShapeDtypeStruct((ny, total_x, width), F32),
        ),
        in_specs=[smem] * 4 + [hbm] * 5,
        out_specs=(hbm, hbm, hbm),
        scratch_shapes=[
            pltpu.VMEM(stress.shape, F32),
            pltpu.VMEM(velocity.shape, F32),
            pltpu.VMEM(material.shape, jnp.int32),
            pltpu.VMEM(thigh.shape, BF16),
            pltpu.VMEM(tlow.shape, BF16),
            pltpu.VMEM((4, 2, nz, cy), F32),
            pltpu.VMEM((4, 2, nz, cy), F32),
            pltpu.VMEM((4, cx, cy), F32),
            pltpu.VMEM((4, cx, cy), F32),
            pltpu.VMEM((nz, cx, cy), F32),
            pltpu.VMEM((ny, zc, cx, cy), F32),
            pltpu.VMEM((zc * cx, total_y), BF16),
            pltpu.VMEM((zc * cx, total_y), BF16),
            pltpu.VMEM((total, cx, width), F32),
            pltpu.SemaphoreType.DMA((5,)),
            pltpu.SemaphoreType.DMA((3,)),
            pltpu.SemaphoreType.DMA((8,)),
            pltpu.SemaphoreType.DMA((8,)),
            pltpu.SemaphoreType.DMA((ny,)),
            pltpu.SemaphoreType.DMA((ny,)),
            pltpu.SemaphoreType.DMA((total,)),
            pltpu.SemaphoreType.DMA((total,)),
        ],
        compiler_params=pltpu.CompilerParams(
            collective_id=0, has_side_effects=True, vmem_limit_bytes=56 * 2**20
        ),
        name="elastic_and_lines",
    )(
        buoyancy, lame_first, shear_modulus, piezo,
        stress, velocity, material, jnp.asarray(thigh), jnp.asarray(tlow),
    )

    columns = min(256, total_x)
    wave_x = (2.0 * np.sin(np.pi * np.arange(total_x) / total_x)) ** 2
    wave_y = (2.0 * np.sin(np.pi * np.arange(total_y) / total_y)) ** 2
    wave_y = np.broadcast_to(wave_y.reshape(total, block, 1), (total, block, 128))
    table_spec = pl.BlockSpec((total_x, columns), lambda i: (0, i))
    modes = pl.pallas_call(
        functools.partial(solve_kernel, ny),
        grid=(total_x // columns,),
        out_shape=jax.ShapeDtypeStruct((2, nz, block, total_x), F32),
        in_specs=[smem] * 3
        + [pl.BlockSpec((ny, total_x, width), lambda i: (0, 0, 0))]
        + [table_spec] * 4
        + [
            pl.BlockSpec((1, columns), lambda i: (0, i)),
            pl.BlockSpec((total, block, 128), lambda i: (0, 0, 0)),
        ],
        out_specs=pl.BlockSpec((2, nz, block, columns), lambda i: (0, 0, 0, i)),
        scratch_shapes=[
            pltpu.VMEM((ny * width, total_x), BF16),
            pltpu.VMEM((ny * width, total_x), BF16),
        ],
        compiler_params=pltpu.CompilerParams(vmem_limit_bytes=56 * 2**20),
        name="lines_and_solve",
    )(
        layer_kind, permit_lateral, permit_normal, lines,
        *[jnp.asarray(table) for table in tables_x(total_x)],
        jnp.asarray(wave_x.reshape(1, -1), F32), jnp.asarray(wave_y, F32),
    )
    return stress_next, velocity_next, modes


def solution(mesh):
    cells = P(None, None, "gx", "gy")
    in_specs = (cells, cells, P(None, "gx", "gy")) + (P(),) * 7
    out_specs = (cells, cells, P(None, None, ("gx", "gy"), None))
    return jax.shard_map(
        functools.partial(per_device, mesh.shape["gx"], mesh.shape["gy"]),
        mesh=mesh, in_specs=in_specs, out_specs=out_specs, check_vma=False,
    )
```

```python
import functools
import math

import jax
import jax.numpy as jnp
import ml_dtypes
import numpy as np
from jax import lax
from jax.experimental import pallas as pl
from jax.experimental.pallas import tpu as pltpu
from jax.sharding import PartitionSpec as P

MESH = pl.DeviceIdType.MESH
F32 = jnp.float32
BF16 = jnp.bfloat16


def split_table(table):
    high = table.astype(np.float32).astype(ml_dtypes.bfloat16)
    low = (table - high.astype(np.float64)).astype(np.float32).astype(ml_dtypes.bfloat16)
    return high, low


@functools.lru_cache(maxsize=2)
def tables_y(count_x, count_y, total_y):
    block = total_y // (count_x * count_y)
    half = count_y // 2
    place = np.arange(total_y)
    angle = 2.0 * np.pi / total_y * (place[:, None] * place[None, :] % total_y)
    both = np.stack([np.cos(angle), -np.sin(angle)], axis=1) / math.sqrt(total_y)
    both = both.reshape(total_y, 2, count_x // 2, 2, 2, half, block).transpose(4, 2, 0, 3, 5, 1, 6)
    return split_table(both.reshape(2, count_x // 2, total_y, 4 * half * block))


@functools.lru_cache(maxsize=2)
def tables_x(total_x):
    place = np.arange(total_x)
    angle = 2.0 * np.pi / total_x * (place[:, None] * place[None, :] % total_x)
    scale = 1.0 / math.sqrt(total_x)
    return split_table(np.cos(angle) * scale) + split_table(np.sin(angle) * scale)


def pick(codes, table):
    return jnp.where(codes == 0, table[0], jnp.where(codes == 1, table[1], table[2]))


def dot3(a_high, a_low, b_high, b_low):
    dot = functools.partial(jnp.dot, preferred_element_type=F32)
    return dot(a_high, b_high) + (dot(a_high, b_low) + dot(a_low, b_high))


def step_kernel(
    nx, ny,
    buoy_t, lame_t, shear_t, piezo_t,
    stress_in, veloc_in, mat_in, thigh_in, tlow_in,
    stress_out, veloc_out, lines_out,
    s_ref, v_ref, m_ref, thigh, tlow,
    xs, xr, ys, yr, charge, cols, chigh, clow, sendbuf,
    in_sem, out_sem, own_sem, hsend, hrecv, a_send, a_recv, b_send, b_recv,
):
    gx, gy = lax.axis_index("gx"), lax.axis_index("gy")
    me = gx * ny + gy
    total = nx * ny
    nz, cx, cy = m_ref.shape
    chunks = lines_out.shape[0]
    zc = nz // chunks
    width = lines_out.shape[2] // zc
    half = ny // 2
    side_y = gy // half
    hubs = (half - 1, half)
    is_hub = jnp.logical_or(gy == hubs[0], gy == hubs[1])
    my_hub = half - 1 + side_y

    loads = [
        pltpu.make_async_copy(src, dst, in_sem.at[no])
        for no, (src, dst) in enumerate(
            [(stress_in, s_ref), (veloc_in, v_ref), (mat_in, m_ref), (thigh_in.at[side_y], thigh), (tlow_in.at[side_y], tlow)]
        )
    ]
    for load in loads:
        load.start()

    barrier = pltpu.get_barrier_semaphore()

    def greet(step, carry):
        other = lax.rem(me + step, total)
        pl.semaphore_signal(
            barrier, inc=1, device_id=(other // ny, lax.rem(other, ny)), device_id_type=MESH
        )
        return carry

    lax.fori_loop(1, total, greet, 0)

    row = lax.broadcasted_iota(jnp.int32, (cx, cy), 0)
    lane = lax.broadcasted_iota(jnp.int32, (cx, cy), 1)

    def to_lane(value, source, target):
        return pltpu.roll(value, lax.rem(target - source + cy, cy), 1)

    has = (gx > 0, gx < nx - 1, gy > 0, gy < ny - 1)
    targets = ((gx - 1, gy), (gx + 1, gy), (gx, gy - 1), (gx, gy + 1))
    opposite = (1, 0, 3, 2)

    def halo_copy(turn, side):
        send, recv = (xs, xr) if side < 2 else (ys, yr)
        slot = turn * 2 + side % 2
        return pltpu.make_async_remote_copy(
            src_ref=send.at[slot],
            dst_ref=recv.at[slot],
            send_sem=hsend.at[turn * 4 + side],
            recv_sem=hrecv.at[turn * 4 + side],
            device_id=targets[side],
            device_id_type=MESH,
        )

    def halo_start(turn):
        for side in range(4):
            @pl.when(has[side])
            def _():
                halo_copy(turn, side).start()

    def halo_wait(turn):
        for side in range(4):
            @pl.when(has[side])
            def _():
                halo_copy(turn, side).wait_send()

            @pl.when(has[opposite[side]])
            def _():
                halo_copy(turn, side).wait_recv()

    for side in range(4):
        recv = xr if side < 2 else yr
        for turn in range(2):
            @pl.when(jnp.logical_not(has[opposite[side]]))
            def _():
                recv[turn * 2 + side % 2] = jnp.zeros(recv.shape[1:], F32)

    loads[0].wait()
    xs[0, 0] = s_ref[0, :, 0, :]
    xs[0, 1] = jnp.zeros((nz, cy), F32)
    xs[1, 0] = s_ref[3, :, cx - 1, :]
    xs[1, 1] = s_ref[4, :, cx - 1, :]

    def pack_stress(z, carry):
        low, high = carry
        low = jnp.where(lane == z, to_lane(s_ref[1, z], 0, z), low)
        high = jnp.where(lane == z, to_lane(s_ref[3, z], cy - 1, z), high)
        high = jnp.where(lane == nz + z, to_lane(s_ref[5, z], cy - 1, nz + z), high)
        return low, high

    empty = jnp.zeros((cx, cy), F32)
    low, high = lax.fori_loop(0, nz, pack_stress, (empty, empty))
    ys[0] = low
    ys[1] = high
    pl.semaphore_wait(barrier, total - 1)
    halo_start(0)
    loads[1].wait()
    loads[2].wait()
    halo_wait(0)

    def x_next(value, turn, item, z):
        edge = xr[turn * 2, item, pl.ds(z, 1), :]
        return jnp.where(row == cx - 1, edge, pltpu.roll(value, cx - 1, 0))

    def x_last(value, turn, item, z):
        edge = xr[turn * 2 + 1, item, pl.ds(z, 1), :]
        return jnp.where(row == 0, edge, pltpu.roll(value, 1, 0))

    def y_next(value, turn, item, z):
        edge = to_lane(yr[turn * 2], item * nz + z, cy - 1)
        return jnp.where(lane == cy - 1, edge, pltpu.roll(value, cy - 1, 1))

    def y_last(value, turn, item, z):
        edge = to_lane(yr[turn * 2 + 1], item * nz + z, 0)
        return jnp.where(lane == 0, edge, pltpu.roll(value, 1, 1))

    def above(ref, item, z):
        return jnp.where(z < nz - 1, ref[item, jnp.minimum(z + 1, nz - 1)], 0.0)

    def below(ref, item, z):
        return jnp.where(z > 0, ref[item, jnp.maximum(z - 1, 0)], 0.0)

    def move(z, carry):
        low, high = carry
        buoy = pick(m_ref[z], buoy_t)
        sxx, syy, szz, sxy, sxz, syz = (s_ref[item, z] for item in range(6))
        ux = v_ref[0, z] + buoy * (
            (x_next(sxx, 0, 0, z) - sxx) + (sxy - y_last(sxy, 0, 0, z)) + (sxz - below(s_ref, 4, z))
        )
        uy = v_ref[1, z] + buoy * (
            (sxy - x_last(sxy, 0, 0, z)) + (y_next(syy, 0, 0, z) - syy) + (syz - below(s_ref, 5, z))
        )
        uz = v_ref[2, z] + buoy * (
            (sxz - x_last(sxz, 0, 1, z)) + (syz - y_last(syz, 0, 1, z)) + (above(s_ref, 2, z) - szz)
        )
        v_ref[0, z] = ux
        v_ref[1, z] = uy
        v_ref[2, z] = uz
        low = jnp.where(lane == z, to_lane(ux, 0, z), low)
        low = jnp.where(lane == nz + z, to_lane(uz, 0, nz + z), low)
        high = jnp.where(lane == z, to_lane(uy, cy - 1, z), high)
        return low, high

    low, high = lax.fori_loop(0, nz, move, (empty, empty))
    xs[2, 0] = v_ref[1, :, 0, :]
    xs[2, 1] = v_ref[2, :, 0, :]
    xs[3, 0] = v_ref[0, :, cx - 1, :]
    xs[3, 1] = jnp.zeros((nz, cy), F32)
    ys[2] = low
    ys[3] = high
    halo_start(1)
    save_veloc = pltpu.make_async_copy(v_ref, veloc_out, out_sem.at[0])
    save_veloc.start()
    halo_wait(1)

    def strain(z, carry):
        mat = m_ref[z]
        lame, shear, piezo = pick(mat, lame_t), pick(mat, shear_t), pick(mat, piezo_t)
        ux, uy, uz = v_ref[0, z], v_ref[1, z], v_ref[2, z]
        strain_x = ux - x_last(ux, 1, 0, z)
        strain_y = uy - y_last(uy, 1, 0, z)
        strain_z = uz - below(v_ref, 2, z)
        spread = lame * (strain_x + strain_y + strain_z)
        twice = 2.0 * shear
        s_ref[0, z] = s_ref[0, z] + spread + twice * strain_x
        s_ref[1, z] = s_ref[1, z] + spread + twice * strain_y
        s_ref[2, z] = s_ref[2, z] + spread + twice * strain_z
        s_ref[3, z] = s_ref[3, z] + shear * (
            (y_next(ux, 1, 0, z) - ux) + (x_next(uy, 1, 0, z) - uy)
        )
        sxz = s_ref[4, z] + shear * ((above(v_ref, 0, z) - ux) + (x_next(uz, 1, 1, z) - uz))
        syz = s_ref[5, z] + shear * ((above(v_ref, 1, z) - uy) + (y_next(uz, 1, 1, z) - uz))
        s_ref[4, z] = sxz
        s_ref[5, z] = syz
        charge[z] = piezo * (sxz + syz)
        return carry

    def raw_copy(no, which):
        return pltpu.make_async_remote_copy(
            src_ref=charge.at[pl.ds(no * zc, zc)],
            dst_ref=cols.at[no, gy],
            send_sem=a_send.at[no, which],
            recv_sem=a_recv.at[no, gy],
            device_id=(gx, hubs[which]),
            device_id_type=MESH,
        )

    def arrived_raw(no, source):
        return pltpu.make_async_remote_copy(
            src_ref=charge.at[pl.ds(no * zc, zc)],
            dst_ref=cols.at[no, source],
            send_sem=a_send.at[no, 0],
            recv_sem=a_recv.at[no, source],
            device_id=(gx, source),
            device_id_type=MESH,
        )

    def chunk(no, carry):
        lax.fori_loop(no * zc, no * zc + zc, strain, 0)
        for which in range(2):
            @pl.when(gy != hubs[which])
            def _():
                raw_copy(no, which).start()

        return carry

    lax.fori_loop(0, chunks, chunk, 0)
    save_stress = pltpu.make_async_copy(s_ref, stress_out, out_sem.at[1])
    save_stress.start()

    def store_cols(source, value):
        flat = value.reshape(zc * cx, cy)
        high = flat.astype(BF16)
        where = pl.ds(pl.multiple_of(source * cy, cy), cy)
        chigh[:, where] = high
        clow[:, where] = (flat - high.astype(F32)).astype(BF16)

    loads[3].wait()
    loads[4].wait()
    my_rows = pl.ds(pl.multiple_of(gx * cx, cx), cx)

    def block_copy(no, tx, ty):
        return pltpu.make_async_remote_copy(
            src_ref=sendbuf.at[no, tx * half + ty],
            dst_ref=lines_out.at[no, my_rows, :],
            send_sem=b_send.at[no, tx * half + ty],
            recv_sem=b_recv.at[no, gx],
            device_id=(tx, side_y * half + ty),
            device_id_type=MESH,
        )

    def own_copy(no):
        return pltpu.make_async_copy(
            sendbuf.at[no, gx * half + lax.rem(gy, half)],
            lines_out.at[no, my_rows, :],
            own_sem.at[no],
        )

    def arrived_block(no, source):
        return pltpu.make_async_remote_copy(
            src_ref=sendbuf.at[no, 0],
            dst_ref=lines_out.at[no, pl.ds(pl.multiple_of(source * cx, cx), cx), :],
            send_sem=b_send.at[no, 0],
            recv_sem=b_recv.at[no, source],
            device_id=(source, my_hub),
            device_id_type=MESH,
        )

    def is_me(tx, ty):
        return jnp.logical_and(tx == gx, side_y * half + ty == gy)

    @pl.when(is_hub)
    def _():
        def hub_chunk(no, carry):
            store_cols(gy, charge[pl.ds(no * zc, zc)])

            def take(step, carry):
                source = lax.rem(gy + step, ny)
                arrived_raw(no, source).wait_recv()
                store_cols(source, cols[no, source])
                return carry

            lax.fori_loop(1, ny, take, 0)

            def transform(step, carry):
                pair = lax.rem(gx // 2 + step, nx // 2)
                value = dot3(chigh[...], clow[...], thigh[pair], tlow[pair])
                for i in range(2):
                    for ty in range(half):
                        tx = pair * 2 + i
                        first = (i * half + ty) * width
                        sendbuf[no, tx * half + ty] = jnp.concatenate(
                            [
                                value[z * cx : (z + 1) * cx, first : first + width]
                                for z in range(zc)
                            ],
                            axis=1,
                        )

                        @pl.when(jnp.logical_not(is_me(tx, ty)))
                        def _():
                            block_copy(no, tx, ty).start()

                return carry

            lax.fori_loop(1, nx // 2 + 1, transform, 0)
            own_copy(no).start()
            return carry

        lax.fori_loop(0, chunks, hub_chunk, 0)

        def finish_sends(no, carry):
            own_copy(no).wait()

            def finish_target(tx, carry):
                for ty in range(half):
                    @pl.when(jnp.logical_not(is_me(tx, ty)))
                    def _():
                        block_copy(no, tx, ty).wait_send()

                return carry

            return lax.fori_loop(0, nx, finish_target, carry)

        lax.fori_loop(0, chunks, finish_sends, 0)

    def finish(no, carry):
        for which in range(2):
            @pl.when(gy != hubs[which])
            def _():
                raw_copy(no, which).wait_send()

        def finish_source(source, carry):
            @pl.when(jnp.logical_not(jnp.logical_and(source == gx, is_hub)))
            def _():
                arrived_block(no, source).wait_recv()

            return carry

        return lax.fori_loop(0, nx, finish_source, carry)

    lax.fori_loop(0, chunks, finish, 0)
    save_veloc.wait()
    save_stress.wait()


def solve_kernel(
    ny, kinds, lateral_t, normal_t,
    lines, cos_high, cos_low, sin_high, sin_low, wave_x, wave_y, stress, veloc,
    modes, stress_out, veloc_out, high, low, sem,
):
    me = lax.axis_index("gx") * ny + lax.axis_index("gy")
    width = lines.shape[2]
    _, nz, block, _ = modes.shape
    copies = [
        pltpu.make_async_copy(stress, stress_out, sem.at[0]),
        pltpu.make_async_copy(veloc, veloc_out, sem.at[1]),
    ]

    @pl.when(pl.program_id(0) == 0)
    def _():
        for copy in copies:
            copy.start()
        for source in range(lines.shape[0]):
            value = lines[source].T
            top = value.astype(BF16)
            high[source * width : (source + 1) * width, :] = top
            low[source * width : (source + 1) * width, :] = (value - top.astype(F32)).astype(BF16)

    with_cos = dot3(high[...], low[...], cos_high[...], cos_low[...])
    with_sin = dot3(high[...], low[...], sin_high[...], sin_low[...])

    def part(value, z, no):
        start = (z * 2 + no) * block
        return value[start : start + block]

    lateral = [pick(kinds[z], lateral_t) for z in range(nz)]
    normal = [pick(kinds[z], normal_t) for z in range(nz)]
    couple = [normal[0]] + [0.5 * (normal[z - 1] + normal[z]) for z in range(1, nz)] + [normal[-1]]
    wave = wave_y[me][:, :1] + wave_x[...]
    factors, reals, imags = [], [], []
    for z in range(nz):
        real = part(with_cos, z, 0) + part(with_sin, z, 1)
        imag = part(with_cos, z, 1) - part(with_sin, z, 0)
        pivot = couple[z] + couple[z + 1] + wave * lateral[z]
        if z > 0:
            pivot = pivot - couple[z] * factors[-1]
            real = real + couple[z] * reals[-1]
            imag = imag + couple[z] * imags[-1]
        inverse = 1.0 / pivot
        factors.append(couple[z + 1] * inverse)
        reals.append(real * inverse)
        imags.append(imag * inverse)
    real, imag = reals[-1], imags[-1]
    for z in range(nz - 1, -1, -1):
        if z < nz - 1:
            real = reals[z] + factors[z] * real
            imag = imags[z] + factors[z] * imag
        modes[0, z] = real
        modes[1, z] = imag

    @pl.when(pl.program_id(0) == pl.num_programs(0) - 1)
    def _():
        for copy in copies:
            copy.wait()


def per_device(
    nx, ny, stress, velocity, material, layer_kind,
    buoyancy, lame_first, shear_modulus, piezo, permit_lateral, permit_normal,
):
    nz, cx, cy = material.shape
    total_x, total_y = cx * nx, cy * ny
    total = nx * ny
    block = total_y // total
    zc = max(1, min(nz, 128 // (2 * block)))
    chunks = nz // zc
    width = zc * 2 * block
    smem = pl.BlockSpec(memory_space=pltpu.SMEM)
    hbm = pl.BlockSpec(memory_space=pl.ANY)
    thigh, tlow = tables_y(nx, ny, total_y)
    stress_next, velocity_next, lines = pl.pallas_call(
        functools.partial(step_kernel, nx, ny),
        out_shape=(
            jax.ShapeDtypeStruct(stress.shape, F32),
            jax.ShapeDtypeStruct(velocity.shape, F32),
            jax.ShapeDtypeStruct((chunks, total_x, width), F32),
        ),
        in_specs=[smem] * 4 + [hbm] * 5,
        out_specs=(hbm, hbm, hbm),
        scratch_shapes=[
            pltpu.VMEM(stress.shape, F32),
            pltpu.VMEM(velocity.shape, F32),
            pltpu.VMEM(material.shape, jnp.int32),
            pltpu.VMEM(thigh.shape[1:], BF16),
            pltpu.VMEM(tlow.shape[1:], BF16),
            pltpu.VMEM((4, 2, nz, cy), F32),
            pltpu.VMEM((4, 2, nz, cy), F32),
            pltpu.VMEM((4, cx, cy), F32),
            pltpu.VMEM((4, cx, cy), F32),
            pltpu.VMEM((nz, cx, cy), F32),
            pltpu.VMEM((chunks, ny, zc, cx, cy), F32),
            pltpu.VMEM((zc * cx, total_y), BF16),
            pltpu.VMEM((zc * cx, total_y), BF16),
            pltpu.VMEM((chunks, total // 2, cx, width), F32),
            pltpu.SemaphoreType.DMA((5,)),
            pltpu.SemaphoreType.DMA((2,)),
            pltpu.SemaphoreType.DMA((chunks,)),
            pltpu.SemaphoreType.DMA((8,)),
            pltpu.SemaphoreType.DMA((8,)),
            pltpu.SemaphoreType.DMA((chunks, 2)),
            pltpu.SemaphoreType.DMA((chunks, ny)),
            pltpu.SemaphoreType.DMA((chunks, total // 2)),
            pltpu.SemaphoreType.DMA((chunks, nx)),
        ],
        compiler_params=pltpu.CompilerParams(
            collective_id=0, has_side_effects=True, vmem_limit_bytes=56 * 2**20
        ),
        name="elastic_and_lines",
    )(
        buoyancy, lame_first, shear_modulus, piezo,
        stress, velocity, material, jnp.asarray(thigh), jnp.asarray(tlow),
    )

    columns = min(256, total_x)
    wave_x = (2.0 * np.sin(np.pi * np.arange(total_x) / total_x)) ** 2
    wave_y = (2.0 * np.sin(np.pi * np.arange(total_y) / total_y)) ** 2
    wave_y = np.broadcast_to(wave_y.reshape(total, block, 1), (total, block, 128))
    table_spec = pl.BlockSpec((total_x, columns), lambda i: (0, i))
    modes, stress_next, velocity_next = pl.pallas_call(
        functools.partial(solve_kernel, ny),
        grid=(total_x // columns,),
        out_shape=(
            jax.ShapeDtypeStruct((2, nz, block, total_x), F32),
            jax.ShapeDtypeStruct(stress.shape, F32),
            jax.ShapeDtypeStruct(velocity.shape, F32),
        ),
        in_specs=[smem] * 3
        + [pl.BlockSpec((chunks, total_x, width), lambda i: (0, 0, 0))]
        + [table_spec] * 4
        + [
            pl.BlockSpec((1, columns), lambda i: (0, i)),
            pl.BlockSpec((total, block, 128), lambda i: (0, 0, 0)),
            hbm,
            hbm,
        ],
        out_specs=(pl.BlockSpec((2, nz, block, columns), lambda i: (0, 0, 0, i)), hbm, hbm),
        scratch_shapes=[
            pltpu.VMEM((chunks * width, total_x), BF16),
            pltpu.VMEM((chunks * width, total_x), BF16),
            pltpu.SemaphoreType.DMA((2,)),
        ],
        compiler_params=pltpu.CompilerParams(vmem_limit_bytes=56 * 2**20),
        name="lines_and_solve",
    )(
        layer_kind, permit_lateral, permit_normal, lines,
        *[jnp.asarray(table) for table in tables_x(total_x)],
        jnp.asarray(wave_x.reshape(1, -1), F32), jnp.asarray(wave_y, F32),
        stress_next, velocity_next,
    )
    return stress_next, velocity_next, modes


def solution(mesh):
    cells = P(None, None, "gx", "gy")
    in_specs = (cells, cells, P(None, "gx", "gy")) + (P(),) * 7
    out_specs = (cells, cells, P(None, None, ("gx", "gy"), None))
    return jax.shard_map(
        functools.partial(per_device, mesh.shape["gx"], mesh.shape["gy"]),
        mesh=mesh, in_specs=in_specs, out_specs=out_specs, check_vma=False,
    )
```

```python
import functools
import math

import jax
import jax.numpy as jnp
import ml_dtypes
import numpy as np
from jax import lax
from jax.experimental import pallas as pl
from jax.experimental.pallas import tpu as pltpu
from jax.sharding import PartitionSpec as P

MESH = pl.DeviceIdType.MESH
F32 = jnp.float32
BF16 = jnp.bfloat16


def split_table(table):
    high = table.astype(np.float32).astype(ml_dtypes.bfloat16)
    low = (table - high.astype(np.float64)).astype(np.float32).astype(ml_dtypes.bfloat16)
    return high, low


@functools.lru_cache(maxsize=2)
def tables_y(count_x, count_y, total_y):
    block = total_y // (count_x * count_y)
    half = count_y // 2
    place = np.arange(total_y)
    angle = 2.0 * np.pi / total_y * (place[:, None] * place[None, :] % total_y)
    both = np.stack([np.cos(angle), -np.sin(angle)], axis=1) / math.sqrt(total_y)
    both = both.reshape(total_y, 2, count_x // 2, 2, 2, half, block).transpose(4, 2, 0, 3, 5, 1, 6)
    return split_table(both.reshape(2, count_x // 2, total_y, 4 * half * block))


@functools.lru_cache(maxsize=2)
def tables_x(total_x):
    place = np.arange(total_x)
    angle = 2.0 * np.pi / total_x * (place[:, None] * place[None, :] % total_x)
    scale = 1.0 / math.sqrt(total_x)
    return split_table(np.cos(angle) * scale) + split_table(np.sin(angle) * scale)


def pick(codes, table):
    return jnp.where(codes == 0, table[0], jnp.where(codes == 1, table[1], table[2]))


def dot3(a_high, a_low, b_high, b_low):
    dot = functools.partial(jnp.dot, preferred_element_type=F32)
    return dot(a_high, b_high) + (dot(a_high, b_low) + dot(a_low, b_high))


def step_kernel(
    nx, ny,
    buoy_t, lame_t, shear_t, piezo_t,
    stress_in, veloc_in, mat_in, thigh_in, tlow_in,
    stress_out, veloc_out, lines_out,
    s_ref, v_ref, m_ref, thigh, tlow,
    xs, xr, ys, yr, charge, cols, chigh, clow, sendbuf,
    in_sem, out_sem, own_sem, hsend, hrecv, a_send, a_recv, b_send, b_recv,
):
    gx, gy = lax.axis_index("gx"), lax.axis_index("gy")
    me = gx * ny + gy
    total = nx * ny
    nz, cx, cy = m_ref.shape
    chunks = lines_out.shape[0]
    zc = nz // chunks
    width = lines_out.shape[2] // zc
    half = ny // 2
    side_y = gy // half
    hubs = (half - 1, half)
    is_hub = jnp.logical_or(gy == hubs[0], gy == hubs[1])
    my_hub = half - 1 + side_y

    loads = [
        pltpu.make_async_copy(src, dst, in_sem.at[no])
        for no, (src, dst) in enumerate(
            [(stress_in, s_ref), (veloc_in, v_ref), (mat_in, m_ref), (thigh_in.at[side_y], thigh), (tlow_in.at[side_y], tlow)]
        )
    ]
    for load in loads:
        load.start()

    barrier = pltpu.get_barrier_semaphore()

    def greet(step, carry):
        other = lax.rem(me + step, total)
        pl.semaphore_signal(
            barrier, inc=1, device_id=(other // ny, lax.rem(other, ny)), device_id_type=MESH
        )
        return carry

    lax.fori_loop(1, total, greet, 0)

    row = lax.broadcasted_iota(jnp.int32, (cx, cy), 0)
    lane = lax.broadcasted_iota(jnp.int32, (cx, cy), 1)

    def to_lane(value, source, target):
        return pltpu.roll(value, lax.rem(target - source + cy, cy), 1)

    has = (gx > 0, gx < nx - 1, gy > 0, gy < ny - 1)
    targets = ((gx - 1, gy), (gx + 1, gy), (gx, gy - 1), (gx, gy + 1))
    opposite = (1, 0, 3, 2)

    def halo_copy(turn, side):
        send, recv = (xs, xr) if side < 2 else (ys, yr)
        slot = turn * 2 + side % 2
        return pltpu.make_async_remote_copy(
            src_ref=send.at[slot],
            dst_ref=recv.at[slot],
            send_sem=hsend.at[turn * 4 + side],
            recv_sem=hrecv.at[turn * 4 + side],
            device_id=targets[side],
            device_id_type=MESH,
        )

    def sides(turn):
        return (0, 2) if turn == 1 else range(4)

    def halo_start(turn):
        for side in sides(turn):
            @pl.when(has[side])
            def _():
                halo_copy(turn, side).start()

    def halo_wait(turn):
        for side in sides(turn):
            @pl.when(has[side])
            def _():
                halo_copy(turn, side).wait_send()

            @pl.when(has[opposite[side]])
            def _():
                halo_copy(turn, side).wait_recv()

    for side in range(4):
        recv = xr if side < 2 else yr
        for turn in range(3):
            @pl.when(jnp.logical_not(has[opposite[side]]))
            def _():
                recv[turn * 2 + side % 2] = jnp.zeros(recv.shape[1:], F32)

    loads[0].wait()
    xs[0, 0] = s_ref[0, :, 0, :]
    xs[0, 1] = jnp.zeros((nz, cy), F32)
    xs[1, 0] = s_ref[3, :, cx - 1, :]
    xs[1, 1] = s_ref[4, :, cx - 1, :]

    def pack_stress(z, carry):
        low, high = carry
        low = jnp.where(lane == z, to_lane(s_ref[1, z], 0, z), low)
        high = jnp.where(lane == z, to_lane(s_ref[3, z], cy - 1, z), high)
        high = jnp.where(lane == nz + z, to_lane(s_ref[5, z], cy - 1, nz + z), high)
        return low, high

    empty = jnp.zeros((cx, cy), F32)
    low, high = lax.fori_loop(0, nz, pack_stress, (empty, empty))
    ys[0] = low
    ys[1] = high
    pl.semaphore_wait(barrier, total - 1)
    halo_start(0)
    loads[1].wait()
    loads[2].wait()
    halo_wait(0)

    def x_next(value, turn, item, z):
        edge = xr[turn * 2, item, pl.ds(z, 1), :]
        return jnp.where(row == cx - 1, edge, pltpu.roll(value, cx - 1, 0))

    def x_last(value, turn, item, z):
        edge = xr[turn * 2 + 1, item, pl.ds(z, 1), :]
        return jnp.where(row == 0, edge, pltpu.roll(value, 1, 0))

    def y_next(value, turn, item, z):
        edge = to_lane(yr[turn * 2], item * nz + z, cy - 1)
        return jnp.where(lane == cy - 1, edge, pltpu.roll(value, cy - 1, 1))

    def y_last(value, turn, item, z):
        edge = to_lane(yr[turn * 2 + 1], item * nz + z, 0)
        return jnp.where(lane == 0, edge, pltpu.roll(value, 1, 1))

    def above(ref, item, z):
        return jnp.where(z < nz - 1, ref[item, jnp.minimum(z + 1, nz - 1)], 0.0)

    def below(ref, item, z):
        return jnp.where(z > 0, ref[item, jnp.maximum(z - 1, 0)], 0.0)

    def move_z(z, low):
        sxz, syz, szz = s_ref[4, z], s_ref[5, z], s_ref[2, z]
        uz = v_ref[2, z] + pick(m_ref[z], buoy_t) * (
            (sxz - x_last(sxz, 0, 1, z)) + (syz - y_last(syz, 0, 1, z)) + (above(s_ref, 2, z) - szz)
        )
        v_ref[2, z] = uz
        return jnp.where(lane == z, to_lane(uz, 0, z), low)

    low = lax.fori_loop(0, nz, move_z, empty)
    xs[2, 0] = v_ref[2, :, 0, :]
    xs[2, 1] = jnp.zeros((nz, cy), F32)
    ys[2] = low
    halo_start(1)

    def move_xy(z, carry):
        low, high = carry
        buoy = pick(m_ref[z], buoy_t)
        sxx, syy, sxy, sxz, syz = (s_ref[item, z] for item in (0, 1, 3, 4, 5))
        ux = v_ref[0, z] + buoy * (
            (x_next(sxx, 0, 0, z) - sxx) + (sxy - y_last(sxy, 0, 0, z)) + (sxz - below(s_ref, 4, z))
        )
        uy = v_ref[1, z] + buoy * (
            (sxy - x_last(sxy, 0, 0, z)) + (y_next(syy, 0, 0, z) - syy) + (syz - below(s_ref, 5, z))
        )
        v_ref[0, z] = ux
        v_ref[1, z] = uy
        low = jnp.where(lane == z, to_lane(ux, 0, z), low)
        high = jnp.where(lane == z, to_lane(uy, cy - 1, z), high)
        return low, high

    low, high = lax.fori_loop(0, nz, move_xy, (empty, empty))
    xs[4, 0] = v_ref[1, :, 0, :]
    xs[4, 1] = jnp.zeros((nz, cy), F32)
    xs[5, 0] = v_ref[0, :, cx - 1, :]
    xs[5, 1] = jnp.zeros((nz, cy), F32)
    ys[4] = low
    ys[5] = high
    halo_start(2)
    halo_wait(1)

    def strain_z(z, carry):
        mat = m_ref[z]
        shear, piezo = pick(mat, shear_t), pick(mat, piezo_t)
        ux, uy, uz = v_ref[0, z], v_ref[1, z], v_ref[2, z]
        sxz = s_ref[4, z] + shear * ((above(v_ref, 0, z) - ux) + (x_next(uz, 1, 0, z) - uz))
        syz = s_ref[5, z] + shear * ((above(v_ref, 1, z) - uy) + (y_next(uz, 1, 0, z) - uz))
        s_ref[4, z] = sxz
        s_ref[5, z] = syz
        charge[z] = piezo * (sxz + syz)
        return carry

    def strain_xy(z, carry):
        mat = m_ref[z]
        lame, shear = pick(mat, lame_t), pick(mat, shear_t)
        ux, uy, uz = v_ref[0, z], v_ref[1, z], v_ref[2, z]
        along_x = ux - x_last(ux, 2, 0, z)
        along_y = uy - y_last(uy, 2, 0, z)
        along_z = uz - below(v_ref, 2, z)
        spread = lame * (along_x + along_y + along_z)
        twice = 2.0 * shear
        s_ref[0, z] = s_ref[0, z] + spread + twice * along_x
        s_ref[1, z] = s_ref[1, z] + spread + twice * along_y
        s_ref[2, z] = s_ref[2, z] + spread + twice * along_z
        s_ref[3, z] = s_ref[3, z] + shear * (
            (y_next(ux, 2, 0, z) - ux) + (x_next(uy, 2, 0, z) - uy)
        )
        return carry

    def raw_copy(no, which):
        return pltpu.make_async_remote_copy(
            src_ref=charge.at[pl.ds(no * zc, zc)],
            dst_ref=cols.at[no, gy],
            send_sem=a_send.at[no, which],
            recv_sem=a_recv.at[no, gy],
            device_id=(gx, hubs[which]),
            device_id_type=MESH,
        )

    def arrived_raw(no, source):
        return pltpu.make_async_remote_copy(
            src_ref=charge.at[pl.ds(no * zc, zc)],
            dst_ref=cols.at[no, source],
            send_sem=a_send.at[no, 0],
            recv_sem=a_recv.at[no, source],
            device_id=(gx, source),
            device_id_type=MESH,
        )

    def chunk(no, carry):
        lax.fori_loop(no * zc, no * zc + zc, strain_z, 0)
        for which in range(2):
            @pl.when(gy != hubs[which])
            def _():
                raw_copy(no, which).start()

        return carry

    lax.fori_loop(0, chunks, chunk, 0)
    save_veloc = pltpu.make_async_copy(v_ref, veloc_out, out_sem.at[0])
    save_veloc.start()
    halo_wait(2)
    lax.fori_loop(0, nz, strain_xy, 0)
    save_stress = pltpu.make_async_copy(s_ref, stress_out, out_sem.at[1])
    save_stress.start()

    def store_cols(source, value):
        flat = value.reshape(zc * cx, cy)
        high = flat.astype(BF16)
        where = pl.ds(pl.multiple_of(source * cy, cy), cy)
        chigh[:, where] = high
        clow[:, where] = (flat - high.astype(F32)).astype(BF16)

    loads[3].wait()
    loads[4].wait()
    my_rows = pl.ds(pl.multiple_of(gx * cx, cx), cx)

    def block_copy(no, tx, ty):
        return pltpu.make_async_remote_copy(
            src_ref=sendbuf.at[no, tx * half + ty],
            dst_ref=lines_out.at[no, my_rows, :],
            send_sem=b_send.at[no, tx * half + ty],
            recv_sem=b_recv.at[no, gx],
            device_id=(tx, side_y * half + ty),
            device_id_type=MESH,
        )

    def own_copy(no):
        return pltpu.make_async_copy(
            sendbuf.at[no, gx * half + lax.rem(gy, half)],
            lines_out.at[no, my_rows, :],
            own_sem.at[no],
        )

    def arrived_block(no, source):
        return pltpu.make_async_remote_copy(
            src_ref=sendbuf.at[no, 0],
            dst_ref=lines_out.at[no, pl.ds(pl.multiple_of(source * cx, cx), cx), :],
            send_sem=b_send.at[no, 0],
            recv_sem=b_recv.at[no, source],
            device_id=(source, my_hub),
            device_id_type=MESH,
        )

    def is_me(tx, ty):
        return jnp.logical_and(tx == gx, side_y * half + ty == gy)

    @pl.when(is_hub)
    def _():
        def hub_chunk(no, carry):
            store_cols(gy, charge[pl.ds(no * zc, zc)])

            def take(step, carry):
                source = lax.rem(gy + step, ny)
                arrived_raw(no, source).wait_recv()
                store_cols(source, cols[no, source])
                return carry

            lax.fori_loop(1, ny, take, 0)

            def transform(step, carry):
                pair = lax.rem(gx // 2 + step, nx // 2)
                value = dot3(chigh[...], clow[...], thigh[pair], tlow[pair])
                for i in range(2):
                    for ty in range(half):
                        tx = pair * 2 + i
                        first = (i * half + ty) * width
                        sendbuf[no, tx * half + ty] = jnp.concatenate(
                            [
                                value[z * cx : (z + 1) * cx, first : first + width]
                                for z in range(zc)
                            ],
                            axis=1,
                        )

                        @pl.when(jnp.logical_not(is_me(tx, ty)))
                        def _():
                            block_copy(no, tx, ty).start()

                return carry

            lax.fori_loop(1, nx // 2 + 1, transform, 0)
            own_copy(no).start()
            return carry

        lax.fori_loop(0, chunks, hub_chunk, 0)

        def finish_sends(no, carry):
            own_copy(no).wait()

            def finish_target(tx, carry):
                for ty in range(half):
                    @pl.when(jnp.logical_not(is_me(tx, ty)))
                    def _():
                        block_copy(no, tx, ty).wait_send()

                return carry

            return lax.fori_loop(0, nx, finish_target, carry)

        lax.fori_loop(0, chunks, finish_sends, 0)

    def finish(no, carry):
        for which in range(2):
            @pl.when(gy != hubs[which])
            def _():
                raw_copy(no, which).wait_send()

        def finish_source(source, carry):
            @pl.when(jnp.logical_not(jnp.logical_and(source == gx, is_hub)))
            def _():
                arrived_block(no, source).wait_recv()

            return carry

        return lax.fori_loop(0, nx, finish_source, carry)

    lax.fori_loop(0, chunks, finish, 0)
    save_veloc.wait()
    save_stress.wait()


def solve_kernel(
    ny, kinds, lateral_t, normal_t,
    lines, cos_high, cos_low, sin_high, sin_low, wave_x, wave_y, stress, veloc,
    modes, stress_out, veloc_out, high, low, s_ref, v_ref, sem,
):
    me = lax.axis_index("gx") * ny + lax.axis_index("gy")
    width = lines.shape[2]
    _, nz, block, _ = modes.shape
    loads = [
        pltpu.make_async_copy(stress, s_ref, sem.at[0]),
        pltpu.make_async_copy(veloc, v_ref, sem.at[1]),
    ]
    stores = [
        pltpu.make_async_copy(s_ref, stress_out, sem.at[2]),
        pltpu.make_async_copy(v_ref, veloc_out, sem.at[3]),
    ]

    @pl.when(pl.program_id(0) == 0)
    def _():
        for load in loads:
            load.start()
        for source in range(lines.shape[0]):
            value = lines[source].T
            top = value.astype(BF16)
            high[source * width : (source + 1) * width, :] = top
            low[source * width : (source + 1) * width, :] = (value - top.astype(F32)).astype(BF16)

    with_cos = dot3(high[...], low[...], cos_high[...], cos_low[...])
    with_sin = dot3(high[...], low[...], sin_high[...], sin_low[...])

    @pl.when(pl.program_id(0) == 0)
    def _():
        for load, store in zip(loads, stores):
            load.wait()
            store.start()

    def part(value, z, no):
        start = (z * 2 + no) * block
        return value[start : start + block]

    lateral = [pick(kinds[z], lateral_t) for z in range(nz)]
    normal = [pick(kinds[z], normal_t) for z in range(nz)]
    couple = [normal[0]] + [0.5 * (normal[z - 1] + normal[z]) for z in range(1, nz)] + [normal[-1]]
    wave = wave_y[me][:, :1] + wave_x[...]
    factors, reals, imags = [], [], []
    for z in range(nz):
        real = part(with_cos, z, 0) + part(with_sin, z, 1)
        imag = part(with_cos, z, 1) - part(with_sin, z, 0)
        pivot = couple[z] + couple[z + 1] + wave * lateral[z]
        if z > 0:
            pivot = pivot - couple[z] * factors[-1]
            real = real + couple[z] * reals[-1]
            imag = imag + couple[z] * imags[-1]
        inverse = 1.0 / pivot
        factors.append(couple[z + 1] * inverse)
        reals.append(real * inverse)
        imags.append(imag * inverse)
    real, imag = reals[-1], imags[-1]
    for z in range(nz - 1, -1, -1):
        if z < nz - 1:
            real = reals[z] + factors[z] * real
            imag = imags[z] + factors[z] * imag
        modes[0, z] = real
        modes[1, z] = imag

    @pl.when(pl.program_id(0) == pl.num_programs(0) - 1)
    def _():
        for store in stores:
            store.wait()


def per_device(
    nx, ny, stress, velocity, material, layer_kind,
    buoyancy, lame_first, shear_modulus, piezo, permit_lateral, permit_normal,
):
    nz, cx, cy = material.shape
    total_x, total_y = cx * nx, cy * ny
    total = nx * ny
    block = total_y // total
    zc = max(1, min(nz, 128 // (2 * block)))
    chunks = nz // zc
    width = zc * 2 * block
    smem = pl.BlockSpec(memory_space=pltpu.SMEM)
    hbm = pl.BlockSpec(memory_space=pl.ANY)
    thigh, tlow = tables_y(nx, ny, total_y)
    stress_next, velocity_next, lines = pl.pallas_call(
        functools.partial(step_kernel, nx, ny),
        out_shape=(
            jax.ShapeDtypeStruct(stress.shape, F32),
            jax.ShapeDtypeStruct(velocity.shape, F32),
            jax.ShapeDtypeStruct((chunks, total_x, width), F32),
        ),
        in_specs=[smem] * 4 + [hbm] * 5,
        out_specs=(hbm, hbm, hbm),
        scratch_shapes=[
            pltpu.VMEM(stress.shape, F32),
            pltpu.VMEM(velocity.shape, F32),
            pltpu.VMEM(material.shape, jnp.int32),
            pltpu.VMEM(thigh.shape[1:], BF16),
            pltpu.VMEM(tlow.shape[1:], BF16),
            pltpu.VMEM((6, 2, nz, cy), F32),
            pltpu.VMEM((6, 2, nz, cy), F32),
            pltpu.VMEM((6, cx, cy), F32),
            pltpu.VMEM((6, cx, cy), F32),
            pltpu.VMEM((nz, cx, cy), F32),
            pltpu.VMEM((chunks, ny, zc, cx, cy), F32),
            pltpu.VMEM((zc * cx, total_y), BF16),
            pltpu.VMEM((zc * cx, total_y), BF16),
            pltpu.VMEM((chunks, total // 2, cx, width), F32),
            pltpu.SemaphoreType.DMA((5,)),
            pltpu.SemaphoreType.DMA((2,)),
            pltpu.SemaphoreType.DMA((chunks,)),
            pltpu.SemaphoreType.DMA((12,)),
            pltpu.SemaphoreType.DMA((12,)),
            pltpu.SemaphoreType.DMA((chunks, 2)),
            pltpu.SemaphoreType.DMA((chunks, ny)),
            pltpu.SemaphoreType.DMA((chunks, total // 2)),
            pltpu.SemaphoreType.DMA((chunks, nx)),
        ],
        compiler_params=pltpu.CompilerParams(
            collective_id=0, has_side_effects=True, vmem_limit_bytes=56 * 2**20
        ),
        name="elastic_and_lines",
    )(
        buoyancy, lame_first, shear_modulus, piezo,
        stress, velocity, material, jnp.asarray(thigh), jnp.asarray(tlow),
    )

    columns = min(512, total_x)
    wave_x = (2.0 * np.sin(np.pi * np.arange(total_x) / total_x)) ** 2
    wave_y = (2.0 * np.sin(np.pi * np.arange(total_y) / total_y)) ** 2
    wave_y = np.broadcast_to(wave_y.reshape(total, block, 1), (total, block, 128))
    table_spec = pl.BlockSpec((total_x, columns), lambda i: (0, i))
    modes, stress_next, velocity_next = pl.pallas_call(
        functools.partial(solve_kernel, ny),
        grid=(total_x // columns,),
        out_shape=(
            jax.ShapeDtypeStruct((2, nz, block, total_x), F32),
            jax.ShapeDtypeStruct(stress.shape, F32),
            jax.ShapeDtypeStruct(velocity.shape, F32),
        ),
        in_specs=[smem] * 3
        + [pl.BlockSpec((chunks, total_x, width), lambda i: (0, 0, 0))]
        + [table_spec] * 4
        + [
            pl.BlockSpec((1, columns), lambda i: (0, i)),
            pl.BlockSpec((total, block, 128), lambda i: (0, 0, 0)),
            hbm,
            hbm,
        ],
        out_specs=(pl.BlockSpec((2, nz, block, columns), lambda i: (0, 0, 0, i)), hbm, hbm),
        scratch_shapes=[
            pltpu.VMEM((chunks * width, total_x), BF16),
            pltpu.VMEM((chunks * width, total_x), BF16),
            pltpu.VMEM(stress.shape, F32),
            pltpu.VMEM(velocity.shape, F32),
            pltpu.SemaphoreType.DMA((4,)),
        ],
        compiler_params=pltpu.CompilerParams(vmem_limit_bytes=56 * 2**20),
        name="lines_and_solve",
    )(
        layer_kind, permit_lateral, permit_normal, lines,
        *[jnp.asarray(table) for table in tables_x(total_x)],
        jnp.asarray(wave_x.reshape(1, -1), F32), jnp.asarray(wave_y, F32),
        stress_next, velocity_next,
    )
    return stress_next, velocity_next, modes


def solution(mesh):
    cells = P(None, None, "gx", "gy")
    in_specs = (cells, cells, P(None, "gx", "gy")) + (P(),) * 7
    out_specs = (cells, cells, P(None, None, ("gx", "gy"), None))
    return jax.shard_map(
        functools.partial(per_device, mesh.shape["gx"], mesh.shape["gy"]),
        mesh=mesh, in_specs=in_specs, out_specs=out_specs, check_vma=False,
    )
```

```python
import functools
import math

import jax
import jax.numpy as jnp
import ml_dtypes
import numpy as np
from jax import lax
from jax.experimental import pallas as pl
from jax.experimental.pallas import tpu as pltpu
from jax.sharding import PartitionSpec as P

MESH = pl.DeviceIdType.MESH
F32 = jnp.float32
BF16 = jnp.bfloat16


def split_table(table):
    high = table.astype(np.float32).astype(ml_dtypes.bfloat16)
    low = (table - high.astype(np.float64)).astype(np.float32).astype(ml_dtypes.bfloat16)
    return high, low


@functools.lru_cache(maxsize=2)
def tables_y(count_x, count_y, total_y):
    block = total_y // (count_x * count_y)
    half = count_y // 2
    place = np.arange(total_y)
    angle = 2.0 * np.pi / total_y * (place[:, None] * place[None, :] % total_y)
    both = np.stack([np.cos(angle), -np.sin(angle)], axis=1) / math.sqrt(total_y)
    both = both.reshape(total_y, 2, count_x // 2, 2, 2, half, block).transpose(4, 2, 0, 3, 5, 1, 6)
    return split_table(both.reshape(2, count_x // 2, total_y, 4 * half * block))


@functools.lru_cache(maxsize=2)
def tables_x(total_x):
    half = total_x // 2
    place = np.arange(total_x)
    angle = 2.0 * np.pi / total_x * (place[:, None] * place[None, :half] % total_x)
    both = np.stack([np.cos(angle), np.sin(angle)]) / math.sqrt(total_x)
    return split_table(both.reshape(2, half, 2, half).transpose(2, 0, 1, 3))


def pick(codes, table):
    return jnp.where(codes == 0, table[0], jnp.where(codes == 1, table[1], table[2]))


def dot3(a_high, a_low, b_high, b_low):
    dot = functools.partial(jnp.dot, preferred_element_type=F32)
    return dot(a_high, b_high) + (dot(a_high, b_low) + dot(a_low, b_high))


def step_kernel(
    nx, ny,
    buoy_t, lame_t, shear_t, piezo_t,
    stress_in, veloc_in, mat_in, thigh_in, tlow_in,
    stress_out, veloc_out, lines_out,
    s_ref, v_ref, m_ref, thigh, tlow,
    xs, xr, ys, yr, charge, cols, chigh, clow, sendbuf,
    in_sem, out_sem, own_sem, hsend, hrecv, a_send, a_recv, b_send, b_recv,
):
    gx, gy = lax.axis_index("gx"), lax.axis_index("gy")
    me = gx * ny + gy
    total = nx * ny
    nz, cx, cy = m_ref.shape
    chunks = lines_out.shape[0]
    zc = nz // chunks
    width = lines_out.shape[2] // zc
    half = ny // 2
    side_y = gy // half
    hubs = (half - 1, half)
    is_hub = jnp.logical_or(gy == hubs[0], gy == hubs[1])
    my_hub = half - 1 + side_y

    loads = [
        pltpu.make_async_copy(src, dst, in_sem.at[no])
        for no, (src, dst) in enumerate(
            [(stress_in, s_ref), (veloc_in, v_ref), (mat_in, m_ref), (thigh_in.at[side_y], thigh), (tlow_in.at[side_y], tlow)]
        )
    ]
    for load in loads:
        load.start()

    barrier = pltpu.get_barrier_semaphore()

    def greet(step, carry):
        other = lax.rem(me + step, total)
        pl.semaphore_signal(
            barrier, inc=1, device_id=(other // ny, lax.rem(other, ny)), device_id_type=MESH
        )
        return carry

    lax.fori_loop(1, total, greet, 0)

    row = lax.broadcasted_iota(jnp.int32, (cx, cy), 0)
    lane = lax.broadcasted_iota(jnp.int32, (cx, cy), 1)

    def to_lane(value, source, target):
        return pltpu.roll(value, lax.rem(target - source + cy, cy), 1)

    has = (gx > 0, gx < nx - 1, gy > 0, gy < ny - 1)
    targets = ((gx - 1, gy), (gx + 1, gy), (gx, gy - 1), (gx, gy + 1))
    opposite = (1, 0, 3, 2)

    def halo_copy(turn, side):
        send, recv = (xs, xr) if side < 2 else (ys, yr)
        slot = turn * 2 + side % 2
        return pltpu.make_async_remote_copy(
            src_ref=send.at[slot],
            dst_ref=recv.at[slot],
            send_sem=hsend.at[turn * 4 + side],
            recv_sem=hrecv.at[turn * 4 + side],
            device_id=targets[side],
            device_id_type=MESH,
        )

    def sides(turn):
        return (0, 2) if turn == 1 else range(4)

    def halo_start(turn):
        for side in sides(turn):
            @pl.when(has[side])
            def _():
                halo_copy(turn, side).start()

    def halo_wait(turn):
        for side in sides(turn):
            @pl.when(has[side])
            def _():
                halo_copy(turn, side).wait_send()

            @pl.when(has[opposite[side]])
            def _():
                halo_copy(turn, side).wait_recv()

    for side in range(4):
        recv = xr if side < 2 else yr
        for turn in range(3):
            @pl.when(jnp.logical_not(has[opposite[side]]))
            def _():
                recv[turn * 2 + side % 2] = jnp.zeros(recv.shape[1:], F32)

    loads[0].wait()
    xs[0, 0] = s_ref[0, :, 0, :]
    xs[0, 1] = jnp.zeros((nz, cy), F32)
    xs[1, 0] = s_ref[3, :, cx - 1, :]
    xs[1, 1] = s_ref[4, :, cx - 1, :]

    def pack_stress(z, carry):
        low, high = carry
        low = jnp.where(lane == z, to_lane(s_ref[1, z], 0, z), low)
        high = jnp.where(lane == z, to_lane(s_ref[3, z], cy - 1, z), high)
        high = jnp.where(lane == nz + z, to_lane(s_ref[5, z], cy - 1, nz + z), high)
        return low, high

    empty = jnp.zeros((cx, cy), F32)
    low, high = lax.fori_loop(0, nz, pack_stress, (empty, empty))
    ys[0] = low
    ys[1] = high
    pl.semaphore_wait(barrier, total - 1)
    halo_start(0)
    loads[1].wait()
    loads[2].wait()
    halo_wait(0)

    def x_next(value, turn, item, z):
        edge = xr[turn * 2, item, pl.ds(z, 1), :]
        return jnp.where(row == cx - 1, edge, pltpu.roll(value, cx - 1, 0))

    def x_last(value, turn, item, z):
        edge = xr[turn * 2 + 1, item, pl.ds(z, 1), :]
        return jnp.where(row == 0, edge, pltpu.roll(value, 1, 0))

    def y_next(value, turn, item, z):
        edge = to_lane(yr[turn * 2], item * nz + z, cy - 1)
        return jnp.where(lane == cy - 1, edge, pltpu.roll(value, cy - 1, 1))

    def y_last(value, turn, item, z):
        edge = to_lane(yr[turn * 2 + 1], item * nz + z, 0)
        return jnp.where(lane == 0, edge, pltpu.roll(value, 1, 1))

    def above(ref, item, z):
        return jnp.where(z < nz - 1, ref[item, jnp.minimum(z + 1, nz - 1)], 0.0)

    def below(ref, item, z):
        return jnp.where(z > 0, ref[item, jnp.maximum(z - 1, 0)], 0.0)

    def move_z(z, low):
        sxz, syz, szz = s_ref[4, z], s_ref[5, z], s_ref[2, z]
        uz = v_ref[2, z] + pick(m_ref[z], buoy_t) * (
            (sxz - x_last(sxz, 0, 1, z)) + (syz - y_last(syz, 0, 1, z)) + (above(s_ref, 2, z) - szz)
        )
        v_ref[2, z] = uz
        return jnp.where(lane == z, to_lane(uz, 0, z), low)

    low = lax.fori_loop(0, nz, move_z, empty)
    xs[2, 0] = v_ref[2, :, 0, :]
    xs[2, 1] = jnp.zeros((nz, cy), F32)
    ys[2] = low
    halo_start(1)

    def move_xy(z, carry):
        low, high = carry
        buoy = pick(m_ref[z], buoy_t)
        sxx, syy, sxy, sxz, syz = (s_ref[item, z] for item in (0, 1, 3, 4, 5))
        ux = v_ref[0, z] + buoy * (
            (x_next(sxx, 0, 0, z) - sxx) + (sxy - y_last(sxy, 0, 0, z)) + (sxz - below(s_ref, 4, z))
        )
        uy = v_ref[1, z] + buoy * (
            (sxy - x_last(sxy, 0, 0, z)) + (y_next(syy, 0, 0, z) - syy) + (syz - below(s_ref, 5, z))
        )
        v_ref[0, z] = ux
        v_ref[1, z] = uy
        low = jnp.where(lane == z, to_lane(ux, 0, z), low)
        high = jnp.where(lane == z, to_lane(uy, cy - 1, z), high)
        return low, high

    low, high = lax.fori_loop(0, nz, move_xy, (empty, empty))
    xs[4, 0] = v_ref[1, :, 0, :]
    xs[4, 1] = jnp.zeros((nz, cy), F32)
    xs[5, 0] = v_ref[0, :, cx - 1, :]
    xs[5, 1] = jnp.zeros((nz, cy), F32)
    ys[4] = low
    ys[5] = high
    halo_start(2)
    halo_wait(1)

    def strain_z(z, carry):
        mat = m_ref[z]
        shear, piezo = pick(mat, shear_t), pick(mat, piezo_t)
        ux, uy, uz = v_ref[0, z], v_ref[1, z], v_ref[2, z]
        sxz = s_ref[4, z] + shear * ((above(v_ref, 0, z) - ux) + (x_next(uz, 1, 0, z) - uz))
        syz = s_ref[5, z] + shear * ((above(v_ref, 1, z) - uy) + (y_next(uz, 1, 0, z) - uz))
        s_ref[4, z] = sxz
        s_ref[5, z] = syz
        charge[z] = piezo * (sxz + syz)
        return carry

    def strain_xy(z, carry):
        mat = m_ref[z]
        lame, shear = pick(mat, lame_t), pick(mat, shear_t)
        ux, uy, uz = v_ref[0, z], v_ref[1, z], v_ref[2, z]
        along_x = ux - x_last(ux, 2, 0, z)
        along_y = uy - y_last(uy, 2, 0, z)
        along_z = uz - below(v_ref, 2, z)
        spread = lame * (along_x + along_y + along_z)
        twice = 2.0 * shear
        s_ref[0, z] = s_ref[0, z] + spread + twice * along_x
        s_ref[1, z] = s_ref[1, z] + spread + twice * along_y
        s_ref[2, z] = s_ref[2, z] + spread + twice * along_z
        s_ref[3, z] = s_ref[3, z] + shear * (
            (y_next(ux, 2, 0, z) - ux) + (x_next(uy, 2, 0, z) - uy)
        )
        return carry

    def raw_copy(no, which):
        return pltpu.make_async_remote_copy(
            src_ref=charge.at[pl.ds(no * zc, zc)],
            dst_ref=cols.at[no, gy],
            send_sem=a_send.at[no, which],
            recv_sem=a_recv.at[no, gy],
            device_id=(gx, hubs[which]),
            device_id_type=MESH,
        )

    def arrived_raw(no, source):
        return pltpu.make_async_remote_copy(
            src_ref=charge.at[pl.ds(no * zc, zc)],
            dst_ref=cols.at[no, source],
            send_sem=a_send.at[no, 0],
            recv_sem=a_recv.at[no, source],
            device_id=(gx, source),
            device_id_type=MESH,
        )

    def raw_start(no):
        for which in range(2):
            @pl.when(gy != hubs[which])
            def _():
                raw_copy(no, which).start()

    def raw_next(no):
        for which in range(2):
            @pl.when(gy != hubs[which])
            def _():
                raw_copy(no, which).wait_send()

        @pl.when(no + 1 < chunks)
        def _():
            raw_start(no + 1)

    def chunk(no, carry):
        lax.fori_loop(no * zc, no * zc + zc, strain_z, 0)

        @pl.when(no == 0)
        def _():
            raw_start(no)

        return carry

    lax.fori_loop(0, chunks, chunk, 0)
    save_veloc = pltpu.make_async_copy(v_ref, veloc_out, out_sem.at[0])
    save_veloc.start()
    halo_wait(2)
    lax.fori_loop(0, nz, strain_xy, 0)
    save_stress = pltpu.make_async_copy(s_ref, stress_out, out_sem.at[1])
    save_stress.start()

    def store_cols(source, value):
        flat = value.reshape(zc * cx, cy)
        high = flat.astype(BF16)
        where = pl.ds(pl.multiple_of(source * cy, cy), cy)
        chigh[:, where] = high
        clow[:, where] = (flat - high.astype(F32)).astype(BF16)

    loads[3].wait()
    loads[4].wait()
    my_rows = pl.ds(pl.multiple_of(gx * cx, cx), cx)

    def block_copy(no, tx, ty):
        return pltpu.make_async_remote_copy(
            src_ref=sendbuf.at[no, tx * half + ty],
            dst_ref=lines_out.at[no, my_rows, :],
            send_sem=b_send.at[no, tx * half + ty],
            recv_sem=b_recv.at[no, gx],
            device_id=(tx, side_y * half + ty),
            device_id_type=MESH,
        )

    def own_copy(no):
        return pltpu.make_async_copy(
            sendbuf.at[no, gx * half + lax.rem(gy, half)],
            lines_out.at[no, my_rows, :],
            own_sem.at[no],
        )

    def arrived_block(no, source):
        return pltpu.make_async_remote_copy(
            src_ref=sendbuf.at[no, 0],
            dst_ref=lines_out.at[no, pl.ds(pl.multiple_of(source * cx, cx), cx), :],
            send_sem=b_send.at[no, 0],
            recv_sem=b_recv.at[no, source],
            device_id=(source, my_hub),
            device_id_type=MESH,
        )

    def is_me(tx, ty):
        return jnp.logical_and(tx == gx, side_y * half + ty == gy)

    @pl.when(is_hub)
    def _():
        def hub_chunk(no, carry):
            raw_next(no)
            store_cols(gy, charge[pl.ds(no * zc, zc)])

            def take(step, carry):
                source = lax.rem(gy + step, ny)
                arrived_raw(no, source).wait_recv()
                store_cols(source, cols[no, source])
                return carry

            lax.fori_loop(1, ny, take, 0)

            def transform(step, carry):
                pair = lax.rem(gx // 2 + step, nx // 2)
                value = dot3(chigh[...], clow[...], thigh[pair], tlow[pair])
                for i in range(2):
                    for ty in range(half):
                        tx = pair * 2 + i
                        first = (i * half + ty) * width
                        sendbuf[no, tx * half + ty] = jnp.concatenate(
                            [
                                value[z * cx : (z + 1) * cx, first : first + width]
                                for z in range(zc)
                            ],
                            axis=1,
                        )

                        @pl.when(jnp.logical_not(is_me(tx, ty)))
                        def _():
                            block_copy(no, tx, ty).start()

                return carry

            lax.fori_loop(1, nx // 2 + 1, transform, 0)
            own_copy(no).start()
            return carry

        lax.fori_loop(0, chunks, hub_chunk, 0)

        def finish_sends(no, carry):
            own_copy(no).wait()

            def finish_target(tx, carry):
                for ty in range(half):
                    @pl.when(jnp.logical_not(is_me(tx, ty)))
                    def _():
                        block_copy(no, tx, ty).wait_send()

                return carry

            return lax.fori_loop(0, nx, finish_target, carry)

        lax.fori_loop(0, chunks, finish_sends, 0)

    @pl.when(jnp.logical_not(is_hub))
    def _():
        def step(no, carry):
            raw_next(no)
            return carry

        lax.fori_loop(0, chunks, step, 0)

    def finish(no, carry):
        def finish_source(source, carry):
            @pl.when(jnp.logical_not(jnp.logical_and(source == gx, is_hub)))
            def _():
                arrived_block(no, source).wait_recv()

            return carry

        return lax.fori_loop(0, nx, finish_source, carry)

    lax.fori_loop(0, chunks, finish, 0)
    save_veloc.wait()
    save_stress.wait()


def solve_kernel(
    ny, kinds, lateral_t, normal_t, wave_x, wave_y,
    lines_in, thigh_in, tlow_in, stress, veloc,
    modes, stress_out, veloc_out,
    lines, thigh, tlow, high, low, s_ref, v_ref, sem,
):
    me = lax.axis_index("gx") * ny + lax.axis_index("gy")
    chunks, total_x, width = lines.shape
    _, nz, block, _ = modes.shape
    loads = [
        pltpu.make_async_copy(src, dst, sem.at[no])
        for no, (src, dst) in enumerate(
            [(lines_in, lines), (thigh_in, thigh), (tlow_in, tlow), (stress, s_ref), (veloc, v_ref)]
        )
    ]
    stores = [
        pltpu.make_async_copy(s_ref, stress_out, sem.at[5]),
        pltpu.make_async_copy(v_ref, veloc_out, sem.at[6]),
    ]
    for load in loads:
        load.start()
    loads[0].wait()
    for source in range(chunks):
        for parity in range(2):
            value = lines[source, pl.ds(parity, total_x // 2, stride=2), :].T
            top = value.astype(BF16)
            high[parity, source * width : (source + 1) * width, :] = top
            low[parity, source * width : (source + 1) * width, :] = (
                value - top.astype(F32)
            ).astype(BF16)
    loads[1].wait()
    loads[2].wait()

    def product(kind):
        even, odd = (
            dot3(high[parity], low[parity], thigh[parity, kind], tlow[parity, kind])
            for parity in range(2)
        )
        return jnp.concatenate([even + odd, even - odd], axis=1)

    with_cos, with_sin = product(0), product(1)
    for load, store in zip(loads[3:], stores):
        load.wait()
        store.start()

    def part(value, z, no):
        start = (z * 2 + no) * block
        return value[start : start + block]

    lateral = [pick(kinds[z], lateral_t) for z in range(nz)]
    normal = [pick(kinds[z], normal_t) for z in range(nz)]
    couple = [normal[0]] + [0.5 * (normal[z - 1] + normal[z]) for z in range(1, nz)] + [normal[-1]]
    wave = wave_y[me][:, :1] + wave_x[...]
    factors, reals, imags = [], [], []
    for z in range(nz):
        real = part(with_cos, z, 0) + part(with_sin, z, 1)
        imag = part(with_cos, z, 1) - part(with_sin, z, 0)
        pivot = couple[z] + couple[z + 1] + wave * lateral[z]
        if z > 0:
            pivot = pivot - couple[z] * factors[-1]
            real = real + couple[z] * reals[-1]
            imag = imag + couple[z] * imags[-1]
        inverse = 1.0 / pivot
        factors.append(couple[z + 1] * inverse)
        reals.append(real * inverse)
        imags.append(imag * inverse)
    real, imag = reals[-1], imags[-1]
    for z in range(nz - 1, -1, -1):
        if z < nz - 1:
            real = reals[z] + factors[z] * real
            imag = imags[z] + factors[z] * imag
        modes[0, z] = real
        modes[1, z] = imag

    for store in stores:
        store.wait()


def per_device(
    nx, ny, stress, velocity, material, layer_kind,
    buoyancy, lame_first, shear_modulus, piezo, permit_lateral, permit_normal,
):
    nz, cx, cy = material.shape
    total_x, total_y = cx * nx, cy * ny
    total = nx * ny
    block = total_y // total
    zc = max(1, min(nz, 128 // (2 * block)))
    chunks = nz // zc
    width = zc * 2 * block
    smem = pl.BlockSpec(memory_space=pltpu.SMEM)
    hbm = pl.BlockSpec(memory_space=pl.ANY)
    thigh, tlow = tables_y(nx, ny, total_y)
    stress_next, velocity_next, lines = pl.pallas_call(
        functools.partial(step_kernel, nx, ny),
        out_shape=(
            jax.ShapeDtypeStruct(stress.shape, F32),
            jax.ShapeDtypeStruct(velocity.shape, F32),
            jax.ShapeDtypeStruct((chunks, total_x, width), F32),
        ),
        in_specs=[smem] * 4 + [hbm] * 5,
        out_specs=(hbm, hbm, hbm),
        scratch_shapes=[
            pltpu.VMEM(stress.shape, F32),
            pltpu.VMEM(velocity.shape, F32),
            pltpu.VMEM(material.shape, jnp.int32),
            pltpu.VMEM(thigh.shape[1:], BF16),
            pltpu.VMEM(tlow.shape[1:], BF16),
            pltpu.VMEM((6, 2, nz, cy), F32),
            pltpu.VMEM((6, 2, nz, cy), F32),
            pltpu.VMEM((6, cx, cy), F32),
            pltpu.VMEM((6, cx, cy), F32),
            pltpu.VMEM((nz, cx, cy), F32),
            pltpu.VMEM((chunks, ny, zc, cx, cy), F32),
            pltpu.VMEM((zc * cx, total_y), BF16),
            pltpu.VMEM((zc * cx, total_y), BF16),
            pltpu.VMEM((chunks, total // 2, cx, width), F32),
            pltpu.SemaphoreType.DMA((5,)),
            pltpu.SemaphoreType.DMA((2,)),
            pltpu.SemaphoreType.DMA((chunks,)),
            pltpu.SemaphoreType.DMA((12,)),
            pltpu.SemaphoreType.DMA((12,)),
            pltpu.SemaphoreType.DMA((chunks, 2)),
            pltpu.SemaphoreType.DMA((chunks, ny)),
            pltpu.SemaphoreType.DMA((chunks, total // 2)),
            pltpu.SemaphoreType.DMA((chunks, nx)),
        ],
        compiler_params=pltpu.CompilerParams(
            collective_id=0, has_side_effects=True, vmem_limit_bytes=56 * 2**20
        ),
        name="elastic_and_lines",
    )(
        buoyancy, lame_first, shear_modulus, piezo,
        stress, velocity, material, jnp.asarray(thigh), jnp.asarray(tlow),
    )

    wave_x = (2.0 * np.sin(np.pi * np.arange(total_x) / total_x)) ** 2
    wave_y = (2.0 * np.sin(np.pi * np.arange(total_y) / total_y)) ** 2
    wave_y = np.broadcast_to(wave_y.reshape(total, block, 1), (total, block, 128))
    vmem = pl.BlockSpec(memory_space=pltpu.VMEM)
    half = total_x // 2
    xhigh, xlow = tables_x(total_x)
    modes, stress_next, velocity_next = pl.pallas_call(
        functools.partial(solve_kernel, ny),
        out_shape=(
            jax.ShapeDtypeStruct((2, nz, block, total_x), F32),
            jax.ShapeDtypeStruct(stress.shape, F32),
            jax.ShapeDtypeStruct(velocity.shape, F32),
        ),
        in_specs=[smem] * 3 + [vmem] * 2 + [hbm] * 5,
        out_specs=(vmem, hbm, hbm),
        scratch_shapes=[
            pltpu.VMEM((chunks, total_x, width), F32),
            pltpu.VMEM(xhigh.shape, BF16),
            pltpu.VMEM(xlow.shape, BF16),
            pltpu.VMEM((2, chunks * width, half), BF16),
            pltpu.VMEM((2, chunks * width, half), BF16),
            pltpu.VMEM(stress.shape, F32),
            pltpu.VMEM(velocity.shape, F32),
            pltpu.SemaphoreType.DMA((7,)),
        ],
        compiler_params=pltpu.CompilerParams(vmem_limit_bytes=56 * 2**20),
        name="lines_and_solve",
    )(
        layer_kind, permit_lateral, permit_normal,
        jnp.asarray(wave_x.reshape(1, -1), F32), jnp.asarray(wave_y, F32),
        lines, jnp.asarray(xhigh), jnp.asarray(xlow), stress_next, velocity_next,
    )
    return stress_next, velocity_next, modes


def solution(mesh):
    cells = P(None, None, "gx", "gy")
    in_specs = (cells, cells, P(None, "gx", "gy")) + (P(),) * 7
    out_specs = (cells, cells, P(None, None, ("gx", "gy"), None))
    return jax.shard_map(
        functools.partial(per_device, mesh.shape["gx"], mesh.shape["gy"]),
        mesh=mesh, in_specs=in_specs, out_specs=out_specs, check_vma=False,
    )
```

```python
import functools
import math

import jax
import jax.numpy as jnp
import ml_dtypes
import numpy as np
from jax import lax
from jax.experimental import pallas as pl
from jax.experimental.pallas import tpu as pltpu
from jax.sharding import PartitionSpec as P

MESH = pl.DeviceIdType.MESH
F32 = jnp.float32
BF16 = jnp.bfloat16


def split_table(table):
    high = table.astype(np.float32).astype(ml_dtypes.bfloat16)
    low = (table - high.astype(np.float64)).astype(np.float32).astype(ml_dtypes.bfloat16)
    return high, low


@functools.lru_cache(maxsize=2)
def tables_y(count_x, count_y, total_y):
    block = total_y // (count_x * count_y)
    half = count_y // 2
    place = np.arange(total_y)
    angle = 2.0 * np.pi / total_y * (place[:, None] * place[None, :] % total_y)
    both = np.stack([np.cos(angle), -np.sin(angle)], axis=1) / math.sqrt(total_y)
    both = both.reshape(total_y, 2, count_x // 2, 2, 2, half, block).transpose(4, 2, 0, 3, 5, 1, 6)
    return split_table(both.reshape(2, count_x // 2, total_y, 4 * half * block))


@functools.lru_cache(maxsize=2)
def tables_x(total_x):
    half = total_x // 2
    place = np.arange(total_x)
    angle = 2.0 * np.pi / total_x * (place[:, None] * place[None, :half] % total_x)
    both = np.stack([np.cos(angle), np.sin(angle)]) / math.sqrt(total_x)
    return split_table(both.reshape(2, half, 2, half).transpose(2, 0, 1, 3))


def pick(codes, table):
    return jnp.where(codes == 0, table[0], jnp.where(codes == 1, table[1], table[2]))


def dot3(a_high, a_low, b_high, b_low):
    dot = functools.partial(jnp.dot, preferred_element_type=F32)
    return dot(a_high, b_high) + (dot(a_high, b_low) + dot(a_low, b_high))


def step_kernel(
    nx, ny,
    buoy_t, lame_t, shear_t, piezo_t,
    stress_in, veloc_in, mat_in, thigh_in, tlow_in,
    stress_out, veloc_out, lines_out,
    s_ref, v_ref, m_ref, thigh, tlow,
    xs, xr, ys, yr, charge, cols, chigh, clow, sendbuf,
    in_sem, out_sem, own_sem, hsend, hrecv, a_send, a_recv, b_send, b_recv,
):
    gx, gy = lax.axis_index("gx"), lax.axis_index("gy")
    me = gx * ny + gy
    total = nx * ny
    nz, cx, cy = m_ref.shape
    chunks = lines_out.shape[0]
    zc = nz // chunks
    width = lines_out.shape[2] // zc
    half = ny // 2
    side_y = gy // half
    hubs = (half - 1, half)
    is_hub = jnp.logical_or(gy == hubs[0], gy == hubs[1])
    my_hub = half - 1 + side_y

    loads = [
        pltpu.make_async_copy(src, dst, in_sem.at[no])
        for no, (src, dst) in enumerate(
            [(stress_in, s_ref), (veloc_in, v_ref), (mat_in, m_ref), (thigh_in.at[side_y], thigh), (tlow_in.at[side_y], tlow)]
        )
    ]
    for load in loads:
        load.start()

    barrier = pltpu.get_barrier_semaphore()

    def greet(step, carry):
        other = lax.rem(me + step, total)
        pl.semaphore_signal(
            barrier, inc=1, device_id=(other // ny, lax.rem(other, ny)), device_id_type=MESH
        )
        return carry

    lax.fori_loop(1, total, greet, 0)

    row = lax.broadcasted_iota(jnp.int32, (cx, cy), 0)
    lane = lax.broadcasted_iota(jnp.int32, (cx, cy), 1)

    def to_lane(value, source, target):
        return pltpu.roll(value, lax.rem(target - source + cy, cy), 1)

    has = (gx > 0, gx < nx - 1, gy > 0, gy < ny - 1)
    targets = ((gx - 1, gy), (gx + 1, gy), (gx, gy - 1), (gx, gy + 1))
    opposite = (1, 0, 3, 2)

    def halo_copy(turn, side):
        send, recv = (xs, xr) if side < 2 else (ys, yr)
        slot = turn * 2 + side % 2
        return pltpu.make_async_remote_copy(
            src_ref=send.at[slot],
            dst_ref=recv.at[slot],
            send_sem=hsend.at[turn * 4 + side],
            recv_sem=hrecv.at[turn * 4 + side],
            device_id=targets[side],
            device_id_type=MESH,
        )

    def sides(turn):
        return (0, 2) if turn == 1 else range(4)

    def halo_start(turn):
        for side in sides(turn):
            @pl.when(has[side])
            def _():
                halo_copy(turn, side).start()

    def halo_wait(turn):
        for side in sides(turn):
            @pl.when(has[side])
            def _():
                halo_copy(turn, side).wait_send()

            @pl.when(has[opposite[side]])
            def _():
                halo_copy(turn, side).wait_recv()

    for side in range(4):
        recv = xr if side < 2 else yr
        for turn in range(3):
            @pl.when(jnp.logical_not(has[opposite[side]]))
            def _():
                recv[turn * 2 + side % 2] = jnp.zeros(recv.shape[1:], F32)

    loads[0].wait()
    xs[0, 0] = s_ref[0, :, 0, :]
    xs[0, 1] = jnp.zeros((nz, cy), F32)
    xs[1, 0] = s_ref[3, :, cx - 1, :]
    xs[1, 1] = s_ref[4, :, cx - 1, :]

    def pack_stress(z, carry):
        low, high = carry
        low = jnp.where(lane == z, to_lane(s_ref[1, z], 0, z), low)
        high = jnp.where(lane == z, to_lane(s_ref[3, z], cy - 1, z), high)
        high = jnp.where(lane == nz + z, to_lane(s_ref[5, z], cy - 1, nz + z), high)
        return low, high

    empty = jnp.zeros((cx, cy), F32)
    low, high = lax.fori_loop(0, nz, pack_stress, (empty, empty))
    ys[0] = low
    ys[1] = high
    pl.semaphore_wait(barrier, total - 1)
    halo_start(0)
    loads[1].wait()
    loads[2].wait()
    halo_wait(0)

    def x_next(value, turn, item, z):
        edge = xr[turn * 2, item, pl.ds(z, 1), :]
        return jnp.where(row == cx - 1, edge, pltpu.roll(value, cx - 1, 0))

    def x_last(value, turn, item, z):
        edge = xr[turn * 2 + 1, item, pl.ds(z, 1), :]
        return jnp.where(row == 0, edge, pltpu.roll(value, 1, 0))

    def y_next(value, turn, item, z):
        edge = to_lane(yr[turn * 2], item * nz + z, cy - 1)
        return jnp.where(lane == cy - 1, edge, pltpu.roll(value, cy - 1, 1))

    def y_last(value, turn, item, z):
        edge = to_lane(yr[turn * 2 + 1], item * nz + z, 0)
        return jnp.where(lane == 0, edge, pltpu.roll(value, 1, 1))

    def above(ref, item, z):
        return jnp.where(z < nz - 1, ref[item, jnp.minimum(z + 1, nz - 1)], 0.0)

    def below(ref, item, z):
        return jnp.where(z > 0, ref[item, jnp.maximum(z - 1, 0)], 0.0)

    def move_z(z, low):
        sxz, syz, szz = s_ref[4, z], s_ref[5, z], s_ref[2, z]
        uz = v_ref[2, z] + pick(m_ref[z], buoy_t) * (
            (sxz - x_last(sxz, 0, 1, z)) + (syz - y_last(syz, 0, 1, z)) + (above(s_ref, 2, z) - szz)
        )
        v_ref[2, z] = uz
        return jnp.where(lane == z, to_lane(uz, 0, z), low)

    low = lax.fori_loop(0, nz, move_z, empty)
    xs[2, 0] = v_ref[2, :, 0, :]
    xs[2, 1] = jnp.zeros((nz, cy), F32)
    ys[2] = low
    halo_start(1)

    def move_xy(z, carry):
        low, high = carry
        buoy = pick(m_ref[z], buoy_t)
        sxx, syy, sxy, sxz, syz = (s_ref[item, z] for item in (0, 1, 3, 4, 5))
        ux = v_ref[0, z] + buoy * (
            (x_next(sxx, 0, 0, z) - sxx) + (sxy - y_last(sxy, 0, 0, z)) + (sxz - below(s_ref, 4, z))
        )
        uy = v_ref[1, z] + buoy * (
            (sxy - x_last(sxy, 0, 0, z)) + (y_next(syy, 0, 0, z) - syy) + (syz - below(s_ref, 5, z))
        )
        v_ref[0, z] = ux
        v_ref[1, z] = uy
        low = jnp.where(lane == z, to_lane(ux, 0, z), low)
        high = jnp.where(lane == z, to_lane(uy, cy - 1, z), high)
        return low, high

    low, high = lax.fori_loop(0, nz, move_xy, (empty, empty))
    xs[4, 0] = v_ref[1, :, 0, :]
    xs[4, 1] = jnp.zeros((nz, cy), F32)
    xs[5, 0] = v_ref[0, :, cx - 1, :]
    xs[5, 1] = jnp.zeros((nz, cy), F32)
    ys[4] = low
    ys[5] = high
    halo_start(2)
    halo_wait(1)

    def strain_z(z, carry):
        mat = m_ref[z]
        shear, piezo = pick(mat, shear_t), pick(mat, piezo_t)
        ux, uy, uz = v_ref[0, z], v_ref[1, z], v_ref[2, z]
        sxz = s_ref[4, z] + shear * ((above(v_ref, 0, z) - ux) + (x_next(uz, 1, 0, z) - uz))
        syz = s_ref[5, z] + shear * ((above(v_ref, 1, z) - uy) + (y_next(uz, 1, 0, z) - uz))
        s_ref[4, z] = sxz
        s_ref[5, z] = syz
        charge[z] = piezo * (sxz + syz)
        return carry

    def strain_xy(z, carry):
        mat = m_ref[z]
        lame, shear = pick(mat, lame_t), pick(mat, shear_t)
        ux, uy, uz = v_ref[0, z], v_ref[1, z], v_ref[2, z]
        along_x = ux - x_last(ux, 2, 0, z)
        along_y = uy - y_last(uy, 2, 0, z)
        along_z = uz - below(v_ref, 2, z)
        spread = lame * (along_x + along_y + along_z)
        twice = 2.0 * shear
        s_ref[0, z] = s_ref[0, z] + spread + twice * along_x
        s_ref[1, z] = s_ref[1, z] + spread + twice * along_y
        s_ref[2, z] = s_ref[2, z] + spread + twice * along_z
        s_ref[3, z] = s_ref[3, z] + shear * (
            (y_next(ux, 2, 0, z) - ux) + (x_next(uy, 2, 0, z) - uy)
        )
        return carry

    def raw_copy(no, which):
        return pltpu.make_async_remote_copy(
            src_ref=charge.at[pl.ds(no * zc, zc)],
            dst_ref=cols.at[no, gy],
            send_sem=a_send.at[no, which],
            recv_sem=a_recv.at[no, gy],
            device_id=(gx, hubs[which]),
            device_id_type=MESH,
        )

    def arrived_raw(no, source):
        return pltpu.make_async_remote_copy(
            src_ref=charge.at[pl.ds(no * zc, zc)],
            dst_ref=cols.at[no, source],
            send_sem=a_send.at[no, 0],
            recv_sem=a_recv.at[no, source],
            device_id=(gx, source),
            device_id_type=MESH,
        )

    def raw_start(no):
        for which in range(2):
            @pl.when(gy != hubs[which])
            def _():
                raw_copy(no, which).start()

    def raw_next(no):
        for which in range(2):
            @pl.when(gy != hubs[which])
            def _():
                raw_copy(no, which).wait_send()

        @pl.when(no + 1 < chunks)
        def _():
            raw_start(no + 1)

    def chunk(no, carry):
        lax.fori_loop(no * zc, no * zc + zc, strain_z, 0)

        @pl.when(no == 0)
        def _():
            raw_start(no)

        return carry

    lax.fori_loop(0, chunks, chunk, 0)
    save_veloc = pltpu.make_async_copy(v_ref, veloc_out, out_sem.at[0])
    save_veloc.start()
    halo_wait(2)
    lax.fori_loop(0, nz, strain_xy, 0)
    save_stress = pltpu.make_async_copy(s_ref, stress_out, out_sem.at[1])
    save_stress.start()

    def store_cols(source, value):
        flat = value.reshape(zc * cx, cy)
        high = flat.astype(BF16)
        where = pl.ds(pl.multiple_of(source * cy, cy), cy)
        chigh[:, where] = high
        clow[:, where] = (flat - high.astype(F32)).astype(BF16)

    loads[3].wait()
    loads[4].wait()
    my_rows = pl.ds(pl.multiple_of(gx * cx, cx), cx)

    def block_copy(no, tx, ty):
        return pltpu.make_async_remote_copy(
            src_ref=sendbuf.at[no, tx * half + ty],
            dst_ref=lines_out.at[no, my_rows, :],
            send_sem=b_send.at[no, tx * half + ty],
            recv_sem=b_recv.at[no, gx],
            device_id=(tx, side_y * half + ty),
            device_id_type=MESH,
        )

    def own_copy(no):
        return pltpu.make_async_copy(
            sendbuf.at[no, gx * half + lax.rem(gy, half)],
            lines_out.at[no, my_rows, :],
            own_sem.at[no],
        )

    def arrived_block(no, source):
        return pltpu.make_async_remote_copy(
            src_ref=sendbuf.at[no, 0],
            dst_ref=lines_out.at[no, pl.ds(pl.multiple_of(source * cx, cx), cx), :],
            send_sem=b_send.at[no, 0],
            recv_sem=b_recv.at[no, source],
            device_id=(source, my_hub),
            device_id_type=MESH,
        )

    def is_me(tx, ty):
        return jnp.logical_and(tx == gx, side_y * half + ty == gy)

    @pl.when(is_hub)
    def _():
        def hub_chunk(no, carry):
            raw_next(no)
            store_cols(gy, charge[pl.ds(no * zc, zc)])

            def take(step, carry):
                source = lax.rem(gy + step, ny)
                arrived_raw(no, source).wait_recv()
                store_cols(source, cols[no, source])
                return carry

            lax.fori_loop(1, ny, take, 0)

            def transform(step, carry):
                pair = lax.rem(gx // 2 + step, nx // 2)
                value = dot3(chigh[...], clow[...], thigh[pair], tlow[pair])
                for i in range(2):
                    for ty in range(half):
                        tx = pair * 2 + i
                        first = (i * half + ty) * width
                        sendbuf[no, tx * half + ty] = jnp.concatenate(
                            [
                                value[z * cx : (z + 1) * cx, first : first + width]
                                for z in range(zc)
                            ],
                            axis=1,
                        )

                        @pl.when(jnp.logical_not(is_me(tx, ty)))
                        def _():
                            block_copy(no, tx, ty).start()

                return carry

            lax.fori_loop(1, nx // 2 + 1, transform, 0)
            own_copy(no).start()
            return carry

        lax.fori_loop(0, chunks, hub_chunk, 0)

        def finish_sends(no, carry):
            own_copy(no).wait()

            def finish_target(tx, carry):
                for ty in range(half):
                    @pl.when(jnp.logical_not(is_me(tx, ty)))
                    def _():
                        block_copy(no, tx, ty).wait_send()

                return carry

            return lax.fori_loop(0, nx, finish_target, carry)

        lax.fori_loop(0, chunks, finish_sends, 0)

    @pl.when(jnp.logical_not(is_hub))
    def _():
        def step(no, carry):
            raw_next(no)
            return carry

        lax.fori_loop(0, chunks, step, 0)

    def finish(no, carry):
        def finish_source(source, carry):
            @pl.when(jnp.logical_not(jnp.logical_and(source == gx, is_hub)))
            def _():
                arrived_block(no, source).wait_recv()

            return carry

        return lax.fori_loop(0, nx, finish_source, carry)

    lax.fori_loop(0, chunks, finish, 0)
    save_veloc.wait()
    save_stress.wait()


def solve_kernel(
    ny, kinds, lateral_t, normal_t, wave_x, wave_y,
    lines_in, thigh_in, tlow_in, stress, veloc,
    modes_out, stress_out, veloc_out,
    modes, lines, thigh, tlow, high, low, s_ref, v_ref, sem, modes_sem,
):
    me = lax.axis_index("gx") * ny + lax.axis_index("gy")
    chunks, total_x, width = lines.shape
    _, nz, block, _ = modes.shape
    loads = [
        pltpu.make_async_copy(src, dst, sem.at[no])
        for no, (src, dst) in enumerate(
            [(lines_in, lines), (thigh_in, thigh), (tlow_in, tlow), (stress, s_ref), (veloc, v_ref)]
        )
    ]
    stores = [
        pltpu.make_async_copy(s_ref, stress_out, sem.at[5]),
        pltpu.make_async_copy(v_ref, veloc_out, sem.at[6]),
    ]
    for load in loads:
        load.start()
    loads[0].wait()
    for source in range(chunks):
        for parity in range(2):
            value = lines[source, pl.ds(parity, total_x // 2, stride=2), :].T
            top = value.astype(BF16)
            high[parity, source * width : (source + 1) * width, :] = top
            low[parity, source * width : (source + 1) * width, :] = (
                value - top.astype(F32)
            ).astype(BF16)
    loads[1].wait()
    loads[2].wait()

    def product(kind):
        even, odd = (
            dot3(high[parity], low[parity], thigh[parity, kind], tlow[parity, kind])
            for parity in range(2)
        )
        return jnp.concatenate([even + odd, even - odd], axis=1)

    with_cos = product(0)
    for load, store in zip(loads[3:], stores):
        load.wait()
        store.start()
    with_sin = product(1)

    def part(value, z, no):
        start = (z * 2 + no) * block
        return value[start : start + block]

    lateral = [pick(kinds[z], lateral_t) for z in range(nz)]
    normal = [pick(kinds[z], normal_t) for z in range(nz)]
    couple = [normal[0]] + [0.5 * (normal[z - 1] + normal[z]) for z in range(1, nz)] + [normal[-1]]
    wave = wave_y[me][:, :1] + wave_x[...]
    factors, reals, imags = [], [], []
    for z in range(nz):
        real = part(with_cos, z, 0) + part(with_sin, z, 1)
        imag = part(with_cos, z, 1) - part(with_sin, z, 0)
        pivot = couple[z] + couple[z + 1] + wave * lateral[z]
        if z > 0:
            pivot = pivot - couple[z] * factors[-1]
            real = real + couple[z] * reals[-1]
            imag = imag + couple[z] * imags[-1]
        inverse = 1.0 / pivot
        factors.append(couple[z + 1] * inverse)
        reals.append(real * inverse)
        imags.append(imag * inverse)
    real, imag = reals[-1], imags[-1]
    for z in range(nz - 1, -1, -1):
        if z < nz - 1:
            real = reals[z] + factors[z] * real
            imag = imags[z] + factors[z] * imag
        modes[0, z] = real
        modes[1, z] = imag
        store = pltpu.make_async_copy(modes.at[:, z], modes_out.at[:, z], modes_sem.at[z])
        store.start()
        stores.append(store)

    for store in stores:
        store.wait()


def per_device(
    nx, ny, stress, velocity, material, layer_kind,
    buoyancy, lame_first, shear_modulus, piezo, permit_lateral, permit_normal,
):
    nz, cx, cy = material.shape
    total_x, total_y = cx * nx, cy * ny
    total = nx * ny
    block = total_y // total
    zc = max(1, min(nz, 128 // (2 * block)))
    chunks = nz // zc
    width = zc * 2 * block
    smem = pl.BlockSpec(memory_space=pltpu.SMEM)
    hbm = pl.BlockSpec(memory_space=pl.ANY)
    thigh, tlow = tables_y(nx, ny, total_y)
    stress_next, velocity_next, lines = pl.pallas_call(
        functools.partial(step_kernel, nx, ny),
        out_shape=(
            jax.ShapeDtypeStruct(stress.shape, F32),
            jax.ShapeDtypeStruct(velocity.shape, F32),
            jax.ShapeDtypeStruct((chunks, total_x, width), F32),
        ),
        in_specs=[smem] * 4 + [hbm] * 5,
        out_specs=(hbm, hbm, hbm),
        scratch_shapes=[
            pltpu.VMEM(stress.shape, F32),
            pltpu.VMEM(velocity.shape, F32),
            pltpu.VMEM(material.shape, jnp.int32),
            pltpu.VMEM(thigh.shape[1:], BF16),
            pltpu.VMEM(tlow.shape[1:], BF16),
            pltpu.VMEM((6, 2, nz, cy), F32),
            pltpu.VMEM((6, 2, nz, cy), F32),
            pltpu.VMEM((6, cx, cy), F32),
            pltpu.VMEM((6, cx, cy), F32),
            pltpu.VMEM((nz, cx, cy), F32),
            pltpu.VMEM((chunks, ny, zc, cx, cy), F32),
            pltpu.VMEM((zc * cx, total_y), BF16),
            pltpu.VMEM((zc * cx, total_y), BF16),
            pltpu.VMEM((chunks, total // 2, cx, width), F32),
            pltpu.SemaphoreType.DMA((5,)),
            pltpu.SemaphoreType.DMA((2,)),
            pltpu.SemaphoreType.DMA((chunks,)),
            pltpu.SemaphoreType.DMA((12,)),
            pltpu.SemaphoreType.DMA((12,)),
            pltpu.SemaphoreType.DMA((chunks, 2)),
            pltpu.SemaphoreType.DMA((chunks, ny)),
            pltpu.SemaphoreType.DMA((chunks, total // 2)),
            pltpu.SemaphoreType.DMA((chunks, nx)),
        ],
        compiler_params=pltpu.CompilerParams(
            collective_id=0, has_side_effects=True, vmem_limit_bytes=56 * 2**20
        ),
        name="elastic_and_lines",
    )(
        buoyancy, lame_first, shear_modulus, piezo,
        stress, velocity, material, jnp.asarray(thigh), jnp.asarray(tlow),
    )

    wave_x = (2.0 * np.sin(np.pi * np.arange(total_x) / total_x)) ** 2
    wave_y = (2.0 * np.sin(np.pi * np.arange(total_y) / total_y)) ** 2
    wave_y = np.broadcast_to(wave_y.reshape(total, block, 1), (total, block, 128))
    vmem = pl.BlockSpec(memory_space=pltpu.VMEM)
    half = total_x // 2
    xhigh, xlow = tables_x(total_x)
    modes, stress_next, velocity_next = pl.pallas_call(
        functools.partial(solve_kernel, ny),
        out_shape=(
            jax.ShapeDtypeStruct((2, nz, block, total_x), F32),
            jax.ShapeDtypeStruct(stress.shape, F32),
            jax.ShapeDtypeStruct(velocity.shape, F32),
        ),
        in_specs=[smem] * 3 + [vmem] * 2 + [hbm] * 5,
        out_specs=(hbm, hbm, hbm),
        scratch_shapes=[
            pltpu.VMEM((2, nz, block, total_x), F32),
            pltpu.VMEM((chunks, total_x, width), F32),
            pltpu.VMEM(xhigh.shape, BF16),
            pltpu.VMEM(xlow.shape, BF16),
            pltpu.VMEM((2, chunks * width, half), BF16),
            pltpu.VMEM((2, chunks * width, half), BF16),
            pltpu.VMEM(stress.shape, F32),
            pltpu.VMEM(velocity.shape, F32),
            pltpu.SemaphoreType.DMA((7,)),
            pltpu.SemaphoreType.DMA((nz,)),
        ],
        compiler_params=pltpu.CompilerParams(vmem_limit_bytes=56 * 2**20),
        name="lines_and_solve",
    )(
        layer_kind, permit_lateral, permit_normal,
        jnp.asarray(wave_x.reshape(1, -1), F32), jnp.asarray(wave_y, F32),
        lines, jnp.asarray(xhigh), jnp.asarray(xlow), stress_next, velocity_next,
    )
    return stress_next, velocity_next, modes


def solution(mesh):
    cells = P(None, None, "gx", "gy")
    in_specs = (cells, cells, P(None, "gx", "gy")) + (P(),) * 7
    out_specs = (cells, cells, P(None, None, ("gx", "gy"), None))
    return jax.shard_map(
        functools.partial(per_device, mesh.shape["gx"], mesh.shape["gy"]),
        mesh=mesh, in_specs=in_specs, out_specs=out_specs, check_vma=False,
    )
```
